512 devices in a mesh: group: 16 (over x, y_hi, core), tensor: 32 (over z, y_lo).
Axes of the slice: x: 4, y: 4 (y_hi: 2, y_lo: 2; y = y_hi * 2 + y_lo), z: 16, core: 2. Of those that a mesh axis runs over, the one named last changes fastest.
Arguments:
- x_prompt: bfloat16 [2048, 16384], P('group', 'tensor'), may hold values from -6 to 6
- z_prompt: bfloat16 [2048, 16384], P('group', 'tensor'), may hold values from -6 to 6
- conv_weight: bfloat16 [4, 16384], P(None, 'tensor'), may hold values from -3 to 3
- conv_bias: bfloat16 [16384], P('tensor'), may hold values from -0.5 to 0.5
- xproj_weight: bfloat16 [16384, 544], P('tensor'), may hold values from -0.046875 to 0.046875
- dtproj_weight: bfloat16 [512, 16384], P(None, 'tensor'), may hold values from -0.25 to 0.25
- dt_bias: float32 [16384], P('tensor'), may hold values from -7 to -2.5
- decay_rate: float32 [16384, 16], P('tensor'), may hold values from 0.5 to 16
- skip_gain: float32 [16384], P('tensor'), may hold values from 0.5 to 1.5
- sample_prompt: int32 [32], P('group'), may hold values from 0 to 1, as said below
- decode_x: bfloat16 [4, 32, 16384], P(None, 'group', 'tensor'), may hold values from -6 to 6
- decode_z: bfloat16 [4, 32, 16384], P(None, 'group', 'tensor'), may hold values from -6 to 6
Outputs:
- prompt_out: bfloat16 [2048, 16384], P('group', 'tensor')
- decode_out: bfloat16 [4, 32, 16384], P(None, 'group', 'tensor')
The draws below stay inside these ranges and needn't reach their ends.
Inputs may be any that keep to these rules, and one draw needn't show every extreme that they name: `sample_prompt`: every prompt is continued by exactly 16 samples.
All inputs are finite; a program needn't handle non-finite values.
Results may differ from the reference program's by a relative error of at most 0.013.
Values may be sent and summed in bfloat16 or wider, within the bound.
No kernel may reach another device: no remote copies, remote signals or barrier semaphores. Data moves between devices by JAX's collectives and lax.ppermute only.
A program may use at most 64 MiB of HBM per device.

```python
import math
import jax
import jax.numpy as jnp
from jax import lax

DI = 16384
N = 16
R = 512
KCONV = 4
FORK = 16
STEPS = 4
LEN = 1024
PROMPTS = 2
TOKENS = 2048
SAMPLES = 32


def draw_sample_prompt(key, part):
    key = jax.random.fold_in(key, 7)
    owners = jnp.arange(SAMPLES, dtype=jnp.int32) // FORK
    return jax.random.permutation(key, owners)


def shard_levels(rng, shape, pieces, low, top_value):
    def one(position, blocks):
        draws = jax.random.uniform(jax.random.fold_in(jax.random.fold_in(rng, 6), position), (blocks,), jnp.float32, low / len(pieces), top_value / len(pieces))
        return jnp.repeat(jnp.exp(draws), shape[position] // blocks).reshape((-1,) + (1,) * (len(shape) - position - 1))

    factor_of = one(*pieces[0])
    for cut in pieces[1:]:
        factor_of = factor_of * one(*cut)
    return factor_of


def noise(own_key, shape, spread, reach, cuts=(), kind=jnp.bfloat16):
    loudness = shard_levels(own_key, shape, cuts, -0.22, 0.18) if cuts else 1.0
    drawn = jax.random.normal(own_key, shape, jnp.float32) * spread * loudness
    return jnp.minimum(jnp.maximum(drawn, -reach), reach).astype(kind)


def setup_inputs(seed: int = 0) -> dict:
    key_of = jax.random.split(jax.random.key(seed), 13)
    x_prompt = noise(key_of[0], (TOKENS, DI), 1.0, 6.0, ((0, 16), (1, 32)))
    z_prompt = noise(key_of[1], (TOKENS, DI), 1.0, 6.0, ((0, 16), (1, 32)))
    conv_weight = noise(key_of[2], (KCONV, DI), KCONV ** -0.5, 3.0, ((1, 32),))
    conv_bias = jnp.clip(jax.random.uniform(key_of[3], (DI,), jnp.float32, -0.5, 0.5) * shard_levels(key_of[3], (DI,), ((0, 32),), -0.4, 0.0), -0.5, 0.5).astype(jnp.bfloat16)
    xproj_weight = noise(key_of[4], (DI, R + 2 * N), DI ** -0.5, 0.046875, ((0, 32),))
    dtproj_weight = noise(key_of[5], (R, DI), R ** -0.5, 0.25, ((1, 32),))
    dt_bias = jnp.clip(-7.0 + 4.5 * jax.random.uniform(key_of[6], (DI,), jnp.float32) ** shard_levels(key_of[6], (DI,), ((0, 32),), -0.2, 0.2), -7.0, -2.5)
    decay_rate = jnp.clip(jnp.exp(math.log(16.0) - 3.465736 * jax.random.uniform(key_of[7], (DI, N), jnp.float32) ** shard_levels(key_of[7], (DI, N), ((0, 32),), -0.2, 0.2)), 0.5, 16.0)
    skip_gain = jnp.clip(0.5 + 1.0 * jax.random.uniform(key_of[8], (DI,), jnp.float32) ** shard_levels(key_of[8], (DI,), ((0, 32),), -0.2, 0.2), 0.5, 1.5)
    sample_prompt = draw_sample_prompt(jax.random.fold_in(key_of[12], 71), 0)
    decode_x = noise(key_of[10], (STEPS, SAMPLES, DI), 1.0, 6.0, ((1, 16), (2, 32)))
    decode_z = noise(key_of[11], (STEPS, SAMPLES, DI), 1.0, 6.0, ((1, 16), (2, 32)))
    return {"x_prompt": x_prompt, "z_prompt": z_prompt, "conv_weight": conv_weight, "conv_bias": conv_bias, "xproj_weight": xproj_weight, "dtproj_weight": dtproj_weight, "dt_bias": dt_bias, "decay_rate": decay_rate, "skip_gain": skip_gain, "sample_prompt": sample_prompt, "decode_x": decode_x, "decode_z": decode_z}


def reference(x_prompt, z_prompt, conv_weight, conv_bias, xproj_weight, dtproj_weight, dt_bias, decay_rate, skip_gain, sample_prompt, decode_x, decode_z):
    rate = -decay_rate
    taps = conv_weight.astype(jnp.float32)
    bias = conv_bias.astype(jnp.float32)
    xs = x_prompt.reshape(PROMPTS, LEN, DI)
    zs = z_prompt.reshape(PROMPTS, LEN, DI)

    def one_prompt(pair):
        xrow, zrow = pair
        ext = jnp.concatenate([jnp.zeros((KCONV - 1, DI), jnp.float32), xrow.astype(jnp.float32)], 0)
        mixed = bias[None]
        for k in range(KCONV):
            mixed = mixed + taps[k][None] * ext[k:k + LEN]
        conv_in = jax.nn.silu(mixed).astype(jnp.bfloat16)
        proj = jnp.dot(conv_in, xproj_weight, preferred_element_type=jnp.float32)
        dt_low = proj[:, :R].astype(jnp.bfloat16)
        coef_b = proj[:, R:R + N]
        coef_c = proj[:, R + N:]
        step = jax.nn.softplus(jnp.dot(dt_low, dtproj_weight, preferred_element_type=jnp.float32) + dt_bias[None])
        inputs = conv_in.astype(jnp.float32)

        def advance(state, items):
            dt_t, u_t, b_t, c_t = items
            state = jnp.exp(dt_t[:, None] * rate) * state + (dt_t * u_t)[:, None] * b_t[None]
            return state, jnp.dot(state, c_t, precision=lax.Precision.HIGHEST)

        final_state, scan_y = lax.scan(advance, jnp.zeros((DI, N), jnp.float32), (step, inputs, coef_b, coef_c))
        result = (scan_y + skip_gain[None] * inputs) * jax.nn.silu(zrow.astype(jnp.float32))
        return result.astype(jnp.bfloat16), final_state, xrow[LEN - (KCONV - 1):]

    outputs, finals, tails = lax.map(one_prompt, (xs, zs))
    prompt_out = outputs.reshape(TOKENS, DI)
    state = finals[sample_prompt]
    window = jnp.concatenate([tails[sample_prompt].astype(jnp.float32), jnp.transpose(decode_x.astype(jnp.float32), (1, 0, 2))], 1)
    results = []
    for step_index in range(STEPS):
        mixed = bias[None]
        for k in range(KCONV):
            mixed = mixed + taps[k][None] * window[:, step_index + k]
        dec_in = jax.nn.silu(mixed).astype(jnp.bfloat16)
        proj = jnp.dot(dec_in, xproj_weight, preferred_element_type=jnp.float32)
        dec_low = proj[:, :R].astype(jnp.bfloat16)
        dec_b = proj[:, R:R + N]
        dec_c = proj[:, R + N:]
        dec_step = jax.nn.softplus(jnp.dot(dec_low, dtproj_weight, preferred_element_type=jnp.float32) + dt_bias[None])
        inputs = dec_in.astype(jnp.float32)
        state = jnp.exp(dec_step[:, :, None] * rate[None]) * state + (dec_step * inputs)[:, :, None] * dec_b[:, None, :]
        value = jnp.einsum("scn,sn->sc", state, dec_c, precision=lax.Precision.HIGHEST) + skip_gain[None] * inputs
        results.append((value * jax.nn.silu(decode_z[step_index].astype(jnp.float32))).astype(jnp.bfloat16))
    return prompt_out, jnp.stack(results, 0)
```

```python
import jax
import jax.numpy as jnp
from jax import lax
from jax.experimental import pallas as pl
from jax.experimental.pallas import tpu as pltpu
from jax.sharding import PartitionSpec as P

N = 16
R = 512
STEPS = 4
F32 = jnp.float32
BF16 = jnp.bfloat16
WIDE = 640
BLOCKS = 8


def silu(v):
    return v * jax.nn.sigmoid(v)


def softplus(v):
    return jnp.maximum(v, 0.0) + jnp.log1p(jnp.exp(-jnp.abs(v)))


def split_tail(total):
    rows = total.shape[0]
    low = total[:, :R].astype(BF16)
    tail = total[:, R:]
    head = tail.astype(BF16)
    rest = (tail - head.astype(F32)).astype(BF16)
    pad = jnp.zeros((rows, 128 - 4 * N), BF16)
    return low, jnp.concatenate([head, rest, pad], 1)


def conv_proj_kernel(x_ref, w_ref, b_ref, xw_ref, rate_ref, part_ref, cin_ref, nrate_ref, ext):
    rows, width = x_ref.shape
    ext[0:8, :] = jnp.zeros((8, width), F32)
    ext[8 : 8 + rows, :] = x_ref[...].astype(F32)
    w = w_ref[...].astype(F32)
    taps = w.shape[0]
    mixed = b_ref[...].astype(F32)
    for k in range(taps):
        mixed = mixed + w[k : k + 1] * ext[8 - (taps - 1) + k : 8 - (taps - 1) + k + rows, :]
    cin = silu(mixed).astype(BF16)
    cin_ref[...] = cin
    part = jnp.dot(cin, xw_ref[...], preferred_element_type=F32)
    part_ref[:, : R + 2 * N] = part.astype(BF16)
    part_ref[:, R + 2 * N :] = jnp.zeros((rows, WIDE - R - 2 * N), BF16)
    nrate_ref[...] = -jnp.transpose(rate_ref[...])


def middle_kernel(sp_ref, got_ref, tails_ref, x_ref, dx_ref, w_ref, b_ref, xw_ref, msg_ref, ein_ref):
    taps, width = w_ref.shape
    place = lax.axis_index("group")
    position = lax.rem(place, BLOCKS)
    w = w_ref[...].astype(F32)
    bias = b_ref[...].astype(F32)
    total = got_ref[0].astype(F32)
    for k in range(1, BLOCKS):
        total = total + got_ref[k].astype(F32)
    msg_ref[0:16, :] = total.astype(BF16)
    before = tails_ref[jnp.maximum(place - 1, 0)].astype(F32)
    before = jnp.where(position == 0, jnp.zeros_like(before), before)
    near = jnp.concatenate([before, x_ref[0:16, :].astype(F32)[0 : taps - 1]], 0)
    rim = bias
    for k in range(taps):
        rim = rim + w[k : k + 1] * near[k : k + taps - 1]
    first = tails_ref[BLOCKS - 1].astype(F32)
    second = tails_ref[2 * BLOCKS - 1].astype(F32)
    picked = [jnp.where(sp_ref[s] == 0, first, second) for s in range(2)]
    window = [
        jnp.concatenate([picked[0][k : k + 1], picked[1][k : k + 1]], 0) for k in range(taps - 1)
    ] + [dx_ref[t].astype(F32) for t in range(STEPS)]
    lines = []
    for t in range(STEPS):
        mixed = bias
        for k in range(taps):
            mixed = mixed + w[k : k + 1] * window[t + k]
        lines.append(mixed)
    extra = jnp.concatenate(lines + [rim, jnp.zeros((8 - (taps - 1), width), F32)], 0)
    ein = silu(extra).astype(BF16)
    ein_ref[...] = ein
    part = jnp.dot(ein, xw_ref[...], preferred_element_type=F32)
    msg_ref[16:32, : R + 2 * N] = part.astype(BF16)
    msg_ref[16:32, R + 2 * N :] = jnp.zeros((16, WIDE - R - 2 * N), BF16)


def sum_kernel(a_ref, b_ref, c_ref, d_ref, out_ref):
    width = R + 2 * N
    total = (a_ref[:, :width].astype(F32) + b_ref[:, :width].astype(F32)) + (
        c_ref[:, :width].astype(F32) + d_ref[:, :width].astype(F32)
    )
    low, tail = split_tail(total)
    for k in range(out_ref.shape[0]):
        out_ref[k, :, :R] = low
        out_ref[k, :, R:] = tail


def joined(block):
    return block + pltpu.roll(block, 128 - 2 * N, 1)


def scan_kernel(
    all_ref, cin_ref, ein_ref, dtw_ref, db_ref, nrate_ref,
    msg_ref, y_ref, reach_ref, bc_ref, dstep_ref, dbc_ref, u_ref, step_ref, low_ref,
):
    rows, width = cin_ref.shape
    ex = all_ref[0, 16:32, :].astype(F32)
    for k in range(1, BLOCKS):
        ex = ex + all_ref[k, 16:32, :].astype(F32)
    turned = jnp.concatenate([ex[8:16], ex[0:8]], 0)
    head = lax.broadcasted_iota(jnp.int32, (16, 1), 0) < 3
    for k in range(BLOCKS):
        low_ref[16 * k : 16 * k + 16, :] = all_ref[k, 0:16, :R]
        bc_ref[16 * k : 16 * k + 16, :] = joined(all_ref[k, 0:16, R:].astype(F32))
    low_ref[0:16, :] = jnp.where(head, turned[:, :R], all_ref[0, 0:16, :R].astype(F32)).astype(BF16)
    bc_ref[0:16, :] = jnp.where(head, joined(turned[:, R:]), bc_ref[0:16, :])
    low_ref[rows : rows + 16, :] = ex[:, :R].astype(BF16)
    step = softplus(
        jnp.dot(low_ref[...], dtw_ref[...], preferred_element_type=F32) + db_ref[...]
    )
    step_ref[...] = step[:rows]
    dstep_ref[...] = step[rows : rows + 8]
    dbc_ref[...] = jnp.transpose(
        jnp.concatenate([joined(ex[:, R:]), jnp.zeros((112, 128), F32)], 0)
    )[0 : 2 * N]
    u_ref[...] = step[:rows] * cin_ref[...].astype(F32)
    ein = ein_ref[...].astype(F32)
    u_ref[0:8, :] = jnp.where(head[0:8], step[0:8] * ein[8:16], u_ref[0:8, :])
    bct = jnp.transpose(bc_ref[...])[0 : 2 * N]
    nrate = nrate_ref[...]

    def group(g, carry):
        h, bc, total = carry
        at = pl.ds(pl.multiple_of(8 * g, 8), 8)
        d8 = step_ref[at, :]
        u8 = u_ref[at, :]
        values, sums = [], []
        for j in range(8):
            d = d8[j : j + 1]
            h = jnp.exp(nrate * d) * h + bc[0:N, j : j + 1] * u8[j : j + 1]
            values.append(jnp.sum(bc[N : 2 * N, j : j + 1] * h, axis=0, keepdims=True))
            total = total + d
            sums.append(total)
        y_ref[at, :] = jnp.concatenate(values, 0)
        reach_ref[at, :] = jnp.concatenate(sums, 0)
        return h, pltpu.roll(bc, 120, 1), total

    h, _, total = lax.fori_loop(
        0, rows // 8, group, (jnp.zeros((N, width), F32), bct, jnp.zeros((1, width), F32))
    )
    lanes = [total[:, 128 * k : 128 * k + 128] for k in range(width // 128)]
    coarse = jnp.concatenate(lanes, 0)
    fine = coarse - coarse.astype(BF16).astype(F32)
    side = jnp.concatenate([coarse, fine, jnp.zeros((8, 128), F32)], 0).astype(BF16)
    for k in range(msg_ref.shape[0]):
        msg_ref[k, :, :width] = h.astype(BF16)
        msg_ref[k, :, width:] = side


def finish_kernel(
    sp_ref, got_ref, y_ref, reach_ref, bc_ref, cin_ref, ein_ref, z_ref, dstep_ref, dbc_ref, dz_ref,
    skip_ref, nrate_ref, out_ref, dec_ref, in_ref,
):
    rows, width = y_ref.shape
    place = lax.axis_index("group")
    mine, position = lax.div(place, BLOCKS), lax.rem(place, BLOCKS)
    nrate = nrate_ref[...]
    skip = skip_ref[...]
    finals = []
    incoming = jnp.zeros((N, width), F32)
    for p in range(2):
        h = jnp.zeros((N, width), F32)
        for k in range(BLOCKS):
            r = p * BLOCKS + k
            if k > 0:
                incoming = jnp.where((mine == p) & (position == k), h, incoming)
            side = got_ref[r, :, width:].astype(F32)
            total = side[0:4] + side[4:8]
            total = jnp.concatenate([total[i : i + 1] for i in range(4)], 1)
            h = jnp.exp(nrate * total) * h + got_ref[r, :, :width].astype(F32)
        finals.append(h)
    in_ref[...] = incoming
    ein = ein_ref[...].astype(F32)

    def group(g, carry):
        at = pl.ds(pl.multiple_of(16 * g, 16), 16)
        s = reach_ref[at, :]
        c = bc_ref[at, :]
        acc = y_ref[at, :]
        for n in range(N):
            acc = acc + c[:, N + n : N + n + 1] * (
                in_ref[n : n + 1, :] * jnp.exp(nrate_ref[n : n + 1, :] * s)
            )
        cin = cin_ref[at, :].astype(F32)
        row = lax.broadcasted_iota(jnp.int32, (16, 1), 0) + 16 * g
        cin = jnp.where(row < 3, jnp.concatenate([ein[8:16], ein[0:8]], 0), cin)
        out_ref[at, :] = ((acc + skip * cin) * silu(z_ref[at, :].astype(F32))).astype(BF16)
        return carry

    lax.fori_loop(0, rows // 16, group, 0)
    states = [jnp.where(sp_ref[s] == 0, finals[0], finals[1]) for s in range(2)]
    for t in range(STEPS):
        values = []
        for s in range(2):
            r = 2 * t + s
            d = dstep_ref[r : r + 1, :]
            u = ein[r : r + 1]
            states[s] = jnp.exp(nrate * d) * states[s] + dbc_ref[0:N, r : r + 1] * (d * u)
            values.append(
                jnp.sum(dbc_ref[N : 2 * N, r : r + 1] * states[s], axis=0, keepdims=True) + skip * u
            )
        value = jnp.concatenate(values, 0) * silu(dz_ref[t].astype(F32))
        dec_ref[t] = value.astype(BF16)


def call(kernel, outs, scratch=(), smem=0, inputs=1, name=None):
    vmem = pl.BlockSpec(memory_space=pltpu.VMEM)
    return pl.pallas_call(
        kernel,
        out_shape=outs,
        in_specs=[pl.BlockSpec(memory_space=pltpu.SMEM)] * smem + [vmem] * inputs,
        out_specs=jax.tree.map(lambda _: vmem, outs),
        scratch_shapes=list(scratch),
        compiler_params=pltpu.CompilerParams(vmem_limit_bytes=48 * 1024 * 1024),
        name=name,
    )


def shape(*dims, kind=F32):
    return jax.ShapeDtypeStruct(dims, kind)


def local(
    x_prompt,
    z_prompt,
    conv_weight,
    conv_bias,
    xproj_weight,
    dtproj_weight,
    dt_bias,
    decay_rate,
    skip_gain,
    sample_prompt,
    decode_x,
    decode_z,
):
    rows, width = x_prompt.shape
    taps = conv_weight.shape[0]
    places = lax.axis_size("group")
    ring = lax.axis_size("tensor")
    bias = conv_bias.reshape(1, width)
    dbias = dt_bias.reshape(1, width)
    skip = skip_gain.reshape(1, width)

    tail = x_prompt[rows - (taps - 1) :]
    tails = lax.all_to_all(
        jnp.broadcast_to(tail[None], (places, taps - 1, width)), "group", 0, 0
    )
    part, cin, nrate = call(
        conv_proj_kernel,
        (shape(rows, WIDE, kind=BF16), shape(rows, width, kind=BF16), shape(N, width)),
        [pltpu.VMEM((rows + 8, width), F32)],
        inputs=5,
        name="conv_proj",
    )(x_prompt, conv_weight, bias, xproj_weight, decay_rate)

    near = [[BLOCKS * a + j for j in range(BLOCKS)] for a in range(ring // BLOCKS)]
    got = lax.all_to_all(
        part.reshape(BLOCKS, rows // BLOCKS, WIDE), "tensor", 0, 0, axis_index_groups=near
    )
    msg, ein = call(
        middle_kernel,
        (shape(32, WIDE, kind=BF16), shape(16, width, kind=BF16)),
        smem=1,
        inputs=7,
        name="middle",
    )(sample_prompt, got, tails, x_prompt, decode_x, conv_weight, bias, xproj_weight)

    others = [
        lax.ppermute(msg, "tensor", [(i, (i + hop) % ring) for i in range(ring)])
        for hop in (2 * BLOCKS, BLOCKS, 3 * BLOCKS)
    ]
    spread = call(
        sum_kernel, shape(BLOCKS, 32, WIDE, kind=BF16), inputs=4, name="sums"
    )(msg, *others)
    everything = lax.all_to_all(spread, "tensor", 0, 0, axis_index_groups=near)

    send, y, reach, bc, dstep, dbc = call(
        scan_kernel,
        (
            shape(places, N, width + 128, kind=BF16),
            shape(rows, width),
            shape(rows, width),
            shape(rows, 128),
            shape(8, width),
            shape(2 * N, 128),
        ),
        [
            pltpu.VMEM((rows, width), F32),
            pltpu.VMEM((rows, width), F32),
            pltpu.VMEM((rows + 16, R), BF16),
        ],
        inputs=6,
        name="scan",
    )(everything, cin, ein, dtproj_weight, dbias, nrate)
    states = lax.all_to_all(send, "group", 0, 0)

    return call(
        finish_kernel,
        (shape(rows, width, kind=BF16), shape(STEPS, 2, width, kind=BF16)),
        [pltpu.VMEM((N, width), F32)],
        smem=1,
        inputs=12,
        name="finish",
    )(sample_prompt, states, y, reach, bc, cin, ein, z_prompt, dstep, dbc, decode_z, skip, nrate)


def solution(mesh):
    placed = (
        P("group", "tensor"),
        P("group", "tensor"),
        P(None, "tensor"),
        P("tensor"),
        P("tensor", None),
        P(None, "tensor"),
        P("tensor"),
        P("tensor", None),
        P("tensor"),
        P("group"),
        P(None, "group", "tensor"),
        P(None, "group", "tensor"),
    )
    return jax.shard_map(
        local,
        mesh=mesh,
        in_specs=placed,
        out_specs=(P("group", "tensor"), P(None, "group", "tensor")),
        check_vma=False,
    )
```

```python
import jax
import jax.numpy as jnp
from jax import lax
from jax.experimental import pallas as pl
from jax.experimental.pallas import tpu as pltpu
from jax.sharding import PartitionSpec as P

N = 16
R = 512
STEPS = 4
F32 = jnp.float32
BF16 = jnp.bfloat16
WIDE = 640
BLOCKS = 8
NEAR = 8


def silu(v):
    return v * jax.nn.sigmoid(v)


def softplus(v):
    return jnp.maximum(v, 0.0) + jnp.log1p(jnp.exp(-jnp.abs(v)))


def folded(tile, line):
    lane = lax.broadcasted_iota(jnp.int32, tile.shape, 1)
    four = jnp.concatenate([line[:, 128 * i : 128 * i + 128] for i in range(4)], 0)
    last = pltpu.roll(line[:, R:], 64, 1)
    side = jnp.concatenate([pltpu.roll(four, 64, 1), four, last, jnp.zeros((7, 128), F32)], 0)
    return jnp.where(lane < 64, tile, side)


def unfolded(tile):
    lane = lax.broadcasted_iota(jnp.int32, (4, 128), 1)
    four = jnp.where(lane < 64, pltpu.roll(tile[0:4], 64, 1), tile[4:8])
    return jnp.concatenate([four[i : i + 1] for i in range(4)], 1), pltpu.roll(tile[8:9], 64, 1)


def with_rest(tile):
    lane = lax.broadcasted_iota(jnp.int32, tile.shape, 1)
    row = lax.broadcasted_iota(jnp.int32, tile.shape, 0)
    head = tile.astype(BF16).astype(F32)
    rest = pltpu.roll(tile - head, 2 * N, 1)
    plain = (lax.rem(lane, 64) < 2 * N) | ((lane >= 64) & (row < 8))
    return jnp.where(plain, head, rest)


def joined(block):
    return block + pltpu.roll(block, 128 - 2 * N, 1)


def onto(rows, columns_ref):
    return lax.dot_general(
        rows, columns_ref[...], (((1,), (1,)), ((), ())), preferred_element_type=F32
    )


def edge_kernel(x_ref, out_ref):
    rows = x_ref.shape[0]
    tail = x_ref[rows - 16 :, :].astype(F32)[8:].astype(BF16)
    for k in range(out_ref.shape[0]):
        out_ref[k] = tail


def prepare_kernel(
    sp_ref, x_ref, w_ref, b_ref, rate_ref, z_ref, dz_ref, db_ref, skip_ref,
    cin_ref, nrate_ref, gate_ref, small_ref, ext,
):
    rows, width = x_ref.shape
    ext[0:8, :] = jnp.zeros((8, width), F32)
    ext[8 : 8 + rows, :] = x_ref[...].astype(F32)
    w = w_ref[...].astype(F32)
    taps = w.shape[0]
    bias = b_ref[...].astype(F32).reshape(1, width)
    mixed = bias
    for k in range(taps):
        mixed = mixed + w[k : k + 1] * ext[9 - taps + k : 9 - taps + k + rows, :]
    cin_ref[...] = silu(mixed).astype(BF16)
    nrate_ref[...] = -rate_ref[...]
    gate_ref[...] = silu(z_ref[...].astype(F32))
    small_ref[0:8, :] = jnp.concatenate(
        [
            db_ref[...].reshape(1, width),
            skip_ref[...].reshape(1, width),
            bias,
            jnp.zeros((1, width), F32),
            w,
        ],
        0,
    )
    for s in range(2):
        small_ref[16 + s : 17 + s, :] = jnp.full((1, width), sp_ref[s], jnp.int32).astype(F32)
    small_ref[8:16, :] = silu(jnp.concatenate([dz_ref[t].astype(F32) for t in range(STEPS)], 0))


def project_kernel(
    tails_ref, cin_ref, x_ref, dx_ref, small_ref, xw_ref, part_ref, all_ref
):
    rows, width = cin_ref.shape
    taps = STEPS
    place = lax.axis_index("group")
    position = lax.rem(place, BLOCKS)
    bias = small_ref[2:3, :]
    w = small_ref[4 : 4 + taps, :]
    before = tails_ref[jnp.maximum(place - 1, 0)].astype(F32)[9 - taps :]
    before = jnp.where(position == 0, jnp.zeros_like(before), before)
    near = jnp.concatenate([before, x_ref[0:16, :].astype(F32)[0 : taps - 1]], 0)
    rim = bias
    for k in range(taps):
        rim = rim + w[k : k + 1] * near[k : k + taps - 1]
    first = tails_ref[BLOCKS - 1].astype(F32)[9 - taps :]
    second = tails_ref[2 * BLOCKS - 1].astype(F32)[9 - taps :]
    picked = [jnp.where(small_ref[16 + s : 17 + s, :] < 0.5, first, second) for s in range(2)]
    window = [
        jnp.concatenate([picked[0][k : k + 1], picked[1][k : k + 1]], 0) for k in range(taps - 1)
    ] + [dx_ref[t].astype(F32) for t in range(STEPS)]
    lines = []
    for t in range(STEPS):
        mixed = bias
        for k in range(taps):
            mixed = mixed + w[k : k + 1] * window[t + k]
        lines.append(mixed)
    extra = silu(jnp.concatenate([rim, jnp.zeros((8 - (taps - 1), width), F32)] + lines, 0))
    row = lax.broadcasted_iota(jnp.int32, (16, 1), 0)
    start = jnp.where(row < taps - 1, extra, cin_ref[0:16, :].astype(F32))
    all_ref[0:16, :] = start.astype(BF16)
    all_ref[16:rows, :] = cin_ref[16:rows, :]
    all_ref[rows : rows + 16, :] = jnp.concatenate(
        [extra[8:16], jnp.zeros((8, width), F32)], 0
    ).astype(BF16)
    part = onto(all_ref[...], xw_ref)
    full = jnp.concatenate([part, jnp.zeros((rows + 16, WIDE - R - 2 * N), F32)], 1)
    for k in range(part_ref.shape[0]):
        mine = full[16 * k : 16 * k + 16]
        part_ref[k, :, :R] = mine[:, :R].astype(BF16)
        part_ref[k, :, R:] = folded(mine[:, R:], full[rows + k : rows + k + 1]).astype(BF16)


def near_sum_kernel(got_ref, out_ref):
    total = got_ref[0].astype(F32)
    for k in range(1, got_ref.shape[0]):
        total = total + got_ref[k].astype(F32)
    total = total.astype(BF16)
    for k in range(out_ref.shape[0]):
        out_ref[k] = total


def far_sum_kernel(got_ref, out_ref):
    total = (got_ref[0].astype(F32) + got_ref[1].astype(F32)) + (
        got_ref[2].astype(F32) + got_ref[3].astype(F32)
    )
    low = total[:, :R].astype(BF16)
    tile = with_rest(total[:, R:]).astype(BF16)
    for k in range(out_ref.shape[0]):
        out_ref[k, :, :R] = low
        out_ref[k, :, R:] = tile


def parts(value):
    head = value.astype(BF16)
    return head, (value - head.astype(F32)).astype(BF16)


def step_kernel(
    all_ref, cin_ref, dtw_ref, small_ref, nrate_ref,
    msg_ref, step_ref, bc_ref, u_ref, dbc_ref, low_ref, left_ref,
):
    rows, width = u_ref.shape
    lines, tiles = [], []
    for k in range(NEAR):
        at = slice(16 * k, 16 * k + 16)
        tile = all_ref[k, :, R:].astype(F32)
        low_ref[at, :] = all_ref[k, :, :R]
        bc_ref[at, :] = joined(tile)
        line, tile = unfolded(tile)
        lines.append(line)
        tiles.append(tile)
    low_ref[rows : rows + 16, :] = jnp.concatenate(
        lines + [jnp.zeros((8, width), F32)], 0
    ).astype(BF16)
    dbc_ref[...] = joined(jnp.concatenate(tiles, 0))
    step = softplus(
        jnp.dot(low_ref[...], dtw_ref[...], preferred_element_type=F32) + small_ref[0:1, :]
    )
    step_ref[...] = step
    step = step[:rows]
    u_ref[...] = step * cin_ref[0:rows, :].astype(F32)
    down = lax.broadcasted_iota(jnp.int32, (rows, rows), 0)
    over = lax.broadcasted_iota(jnp.int32, (rows, rows), 1)
    after = jnp.where(over > down, 1.0, 0.0).astype(BF16)
    left = sum(jnp.dot(after, part, preferred_element_type=F32) for part in parts(step))
    left_ref[...] = left
    ends = []
    for n in range(N):
        rate = nrate_ref[n : n + 1, :]
        acc = jnp.zeros((16, width), F32)
        for g in range(rows // 16):
            at = slice(16 * g, 16 * g + 16)
            acc = acc + jnp.exp(rate * left_ref[at, :]) * (bc_ref[at, n : n + 1] * u_ref[at, :])
        ends.append(jnp.sum(acc, axis=0, keepdims=True))
    total = left[0:1] + step[0:1]
    coarse = jnp.concatenate([total[:, 128 * k : 128 * k + 128] for k in range(width // 128)], 0)
    fine = coarse - coarse.astype(BF16).astype(F32)
    side = jnp.concatenate([coarse, fine, jnp.zeros((8, 128), F32)], 0)
    result = jnp.concatenate([jnp.concatenate(ends, 0), side], 1).astype(BF16)
    for k in range(msg_ref.shape[0]):
        msg_ref[k] = result


def scan_kernel(
    step_ref, u_ref, bc_ref, cin_ref, gate_ref, small_ref, nrate_ref, dbc_ref,
    out_ref, reach_ref, from_ref, dout_ref,
):
    rows, width = u_ref.shape
    down = lax.broadcasted_iota(jnp.int32, (rows, rows), 0)
    over = lax.broadcasted_iota(jnp.int32, (rows, rows), 1)
    upto = jnp.where(over <= down, 1.0, 0.0).astype(BF16)
    reach_ref[...] = sum(
        jnp.dot(upto, part, preferred_element_type=F32) for part in parts(step_ref[0:rows, :])
    )
    dbc = jnp.transpose(jnp.concatenate([dbc_ref[...], jnp.zeros((120, 128), F32)], 0))
    nrate = nrate_ref[...]
    skip = small_ref[1:2, :]
    bct = jnp.transpose(bc_ref[...])[0 : 2 * N]

    def group(g, carry):
        h, bc = carry
        at = pl.ds(pl.multiple_of(8 * g, 8), 8)
        d8 = step_ref[at, :]
        u8 = u_ref[at, :]
        values = []
        for j in range(8):
            h = jnp.exp(nrate * d8[j : j + 1]) * h + bc[0:N, j : j + 1] * u8[j : j + 1]
            values.append(jnp.sum(bc[N : 2 * N, j : j + 1] * h, axis=0, keepdims=True))
        out_ref[at, :] = jnp.concatenate(values, 0)
        return h, pltpu.roll(bc, 120, 1)

    lax.fori_loop(0, rows // 8, group, (jnp.zeros((N, width), F32), bct))
    out_ref[...] = (out_ref[...] + skip * cin_ref[0:rows, :].astype(F32)) * gate_ref[...]
    dec = cin_ref[rows : rows + 16, :].astype(F32)
    own = []
    kept = [jnp.ones((N, width), F32) for _ in range(2)]
    state = [jnp.zeros((N, width), F32) for _ in range(2)]
    for r in range(2 * STEPS):
        s = r % 2
        d = step_ref[rows + r : rows + r + 1, :]
        decay = jnp.exp(nrate * d)
        kept[s] = decay * kept[s]
        state[s] = decay * state[s] + dbc[0:N, r : r + 1] * (d * dec[r : r + 1])
        c = dbc[N : 2 * N, r : r + 1]
        from_ref[r] = c * kept[s]
        own.append(jnp.sum(c * state[s], axis=0, keepdims=True))
    dout_ref[...] = jnp.concatenate(own, 0) + skip * dec[0 : 2 * STEPS]


def finish_kernel(
    sp_ref, got_ref, y_ref, reach_ref, bc_ref, gate_ref, nrate_ref, small_ref, from_ref, own_ref,
    out_ref, dec_ref, in_ref,
):
    rows, width = y_ref.shape
    place = lax.axis_index("group")
    mine, position = lax.div(place, BLOCKS), lax.rem(place, BLOCKS)
    nrate = nrate_ref[...]
    finals = []
    incoming = jnp.zeros((N, width), F32)
    for p in range(2):
        h = jnp.zeros((N, width), F32)
        for k in range(BLOCKS):
            r = p * BLOCKS + k
            if k > 0:
                incoming = jnp.where((mine == p) & (position == k), h, incoming)
            side = got_ref[r, :, width:].astype(F32)
            total = side[0:4] + side[4:8]
            total = jnp.concatenate([total[i : i + 1] for i in range(4)], 1)
            h = jnp.exp(nrate * total) * h + got_ref[r, :, :width].astype(F32)
        finals.append(h)
    in_ref[...] = incoming

    def group(g, carry):
        at = pl.ds(pl.multiple_of(16 * g, 16), 16)
        s = reach_ref[at, :]
        c = bc_ref[at, :]
        acc = jnp.zeros((16, width), F32)
        for n in range(N):
            acc = acc + c[:, N + n : N + n + 1] * (
                in_ref[n : n + 1, :] * jnp.exp(nrate_ref[n : n + 1, :] * s)
            )
        out_ref[at, :] = (y_ref[at, :] + acc * gate_ref[at, :]).astype(BF16)
        return carry

    lax.fori_loop(0, rows // 16, group, 0)
    states = [jnp.where(sp_ref[s] == 0, finals[0], finals[1]) for s in range(2)]
    for t in range(STEPS):
        pair = [
            jnp.sum(from_ref[2 * t + s] * states[s], axis=0, keepdims=True) for s in range(2)
        ]
        at = slice(2 * t, 2 * t + 2)
        value = (jnp.concatenate(pair, 0) + own_ref[at, :]) * small_ref[8 + 2 * t : 10 + 2 * t, :]
        dec_ref[t] = value.astype(BF16)


def call(kernel, outs, scratch=(), smem=0, hbm=0, inputs=0, name=None):
    vmem = pl.BlockSpec(memory_space=pltpu.VMEM)
    return pl.pallas_call(
        kernel,
        out_shape=outs,
        in_specs=[pl.BlockSpec(memory_space=pltpu.SMEM)] * smem
        + [pl.BlockSpec(memory_space=pl.ANY)] * hbm
        + [vmem] * inputs,
        out_specs=jax.tree.map(lambda _: vmem, outs),
        scratch_shapes=list(scratch),
        compiler_params=pltpu.CompilerParams(vmem_limit_bytes=24 * 1024 * 1024),
        name=name,
    )


def shape(*dims, kind=F32):
    return jax.ShapeDtypeStruct(dims, kind)


def local(
    x_prompt,
    z_prompt,
    conv_weight,
    conv_bias,
    xproj_weight,
    dtproj_weight,
    dt_bias,
    decay_rate,
    skip_gain,
    sample_prompt,
    decode_x,
    decode_z,
):
    rows, width = x_prompt.shape
    taps = conv_weight.shape[0]
    places = lax.axis_size("group")
    ring = lax.axis_size("tensor")
    deep = NEAR // 2
    near = [
        [NEAR * a + 2 * ((j + a) % deep) + y for j in range(deep) for y in range(2)]
        for a in range(ring // NEAR)
    ]
    far = [[g[j] for g in near] for j in range(NEAR)]

    tail = call(
        edge_kernel, shape(places, 8, width, kind=BF16), inputs=1, name="edge"
    )(x_prompt)
    tails = lax.all_to_all(tail, "group", 0, 0)
    cin, nrate, gate, small = call(
        prepare_kernel,
        (shape(rows, width, kind=BF16), shape(N, width), shape(rows, width), shape(24, width)),
        [pltpu.VMEM((rows + 8, width), F32)],
        smem=1,
        inputs=8,
        name="prepare",
    )(
        sample_prompt,
        x_prompt,
        conv_weight,
        conv_bias,
        decay_rate.T,
        z_prompt,
        decode_z,
        dt_bias,
        skip_gain,
    )
    part, cin = call(
        project_kernel,
        (shape(NEAR, 16, WIDE, kind=BF16), shape(rows + 16, width, kind=BF16)),
        inputs=6,
        name="project",
    )(tails, cin, x_prompt, decode_x, small, xproj_weight.T)

    got = lax.all_to_all(part, "tensor", 0, 0, axis_index_groups=near)
    sums = call(
        near_sum_kernel, shape(ring // NEAR, 16, WIDE, kind=BF16), inputs=1, name="near_sum"
    )(got)
    got = lax.all_to_all(sums, "tensor", 0, 0, axis_index_groups=far)
    sums = call(far_sum_kernel, shape(NEAR, 16, WIDE, kind=BF16), inputs=1, name="far_sum")(got)
    everything = lax.all_to_all(sums, "tensor", 0, 0, axis_index_groups=near)

    send, step, bc, u, dbc = call(
        step_kernel,
        (
            shape(places, N, width + 128, kind=BF16),
            shape(rows + 16, width),
            shape(rows, 128),
            shape(rows, width),
            shape(8, 128),
        ),
        [pltpu.VMEM((rows + 16, R), BF16), pltpu.VMEM((rows, width), F32)],
        inputs=5,
        name="step",
    )(everything, cin, dtproj_weight, small, nrate)
    states = lax.all_to_all(send, "group", 0, 0)
    y, reach, share, own = call(
        scan_kernel,
        (
            shape(rows, width),
            shape(rows, width),
            shape(2 * STEPS, N, width),
            shape(2 * STEPS, width),
        ),
        inputs=8,
        name="scan",
    )(step, u, bc, cin, gate, small, nrate, dbc)
    return call(
        finish_kernel,
        (shape(rows, width, kind=BF16), shape(STEPS, 2, width, kind=BF16)),
        [pltpu.VMEM((N, width), F32)],
        smem=1,
        inputs=9,
        name="finish",
    )(sample_prompt, states, y, reach, bc, gate, nrate, small, share, own)


def solution(mesh):
    placed = (
        P("group", "tensor"),
        P("group", "tensor"),
        P(None, "tensor"),
        P("tensor"),
        P("tensor", None),
        P(None, "tensor"),
        P("tensor"),
        P("tensor", None),
        P("tensor"),
        P("group"),
        P(None, "group", "tensor"),
        P(None, "group", "tensor"),
    )
    return jax.shard_map(
        local,
        mesh=mesh,
        in_specs=placed,
        out_specs=(P("group", "tensor"), P(None, "group", "tensor")),
        check_vma=False,
    )
```

```python
import jax
import jax.numpy as jnp
from jax import lax
from jax.experimental import pallas as pl
from jax.experimental.pallas import tpu as pltpu
from jax.sharding import PartitionSpec as P

N = 16
R = 512
STEPS = 4
F32 = jnp.float32
BF16 = jnp.bfloat16
WIDE = 640
BLOCKS = 8
NEAR = 8


def silu(v):
    return v * jax.nn.sigmoid(v)


def softplus(v):
    return jnp.maximum(v, 0.0) + jnp.log1p(jnp.exp(-jnp.abs(v)))


def folded(tile, line):
    lane = lax.broadcasted_iota(jnp.int32, tile.shape, 1)
    four = jnp.concatenate([line[:, 128 * i : 128 * i + 128] for i in range(4)], 0)
    last = pltpu.roll(line[:, R:], 64, 1)
    side = jnp.concatenate([pltpu.roll(four, 64, 1), four, last, jnp.zeros((7, 128), F32)], 0)
    return jnp.where(lane < 64, tile, side)


def unfolded(tile):
    lane = lax.broadcasted_iota(jnp.int32, (4, 128), 1)
    four = jnp.where(lane < 64, pltpu.roll(tile[0:4], 64, 1), tile[4:8])
    return jnp.concatenate([four[i : i + 1] for i in range(4)], 1), pltpu.roll(tile[8:9], 64, 1)


def with_rest(tile):
    lane = lax.broadcasted_iota(jnp.int32, tile.shape, 1)
    row = lax.broadcasted_iota(jnp.int32, tile.shape, 0)
    head = tile.astype(BF16).astype(F32)
    rest = pltpu.roll(tile - head, 2 * N, 1)
    plain = (lax.rem(lane, 64) < 2 * N) | ((lane >= 64) & (row < 8))
    return jnp.where(plain, head, rest)


def joined(block):
    return block + pltpu.roll(block, 128 - 2 * N, 1)


def onto(rows, columns_ref):
    return lax.dot_general(
        rows, columns_ref[...], (((1,), (1,)), ((), ())), preferred_element_type=F32
    )


def prepare_kernel(
    sp_ref, x_ref, w_ref, b_ref, xw_ref, rate_ref, z_ref, dz_ref, db_ref, skip_ref,
    part_ref, cin_ref, nrate_ref, gate_ref, small_ref, ext,
):
    rows, width = x_ref.shape
    ext[0:8, :] = jnp.zeros((8, width), F32)
    ext[8 : 8 + rows, :] = x_ref[...].astype(F32)
    w = w_ref[...].astype(F32)
    taps = w.shape[0]
    bias = b_ref[...].astype(F32).reshape(1, width)
    mixed = bias
    for k in range(taps):
        mixed = mixed + w[k : k + 1] * ext[9 - taps + k : 9 - taps + k + rows, :]
    cin = silu(mixed).astype(BF16)
    cin_ref[...] = cin
    part_ref[:, : R + 2 * N] = onto(cin, xw_ref)
    part_ref[:, R + 2 * N :] = jnp.zeros((rows, WIDE - R - 2 * N), F32)
    nrate_ref[...] = -rate_ref[...]
    gate_ref[...] = silu(z_ref[...].astype(F32))
    small_ref[0:8, :] = jnp.concatenate(
        [
            db_ref[...].reshape(1, width),
            skip_ref[...].reshape(1, width),
            bias,
            jnp.zeros((1, width), F32),
            w,
        ],
        0,
    )
    for s in range(2):
        small_ref[16 + s : 17 + s, :] = jnp.full((1, width), sp_ref[s], jnp.int32).astype(F32)
    small_ref[8:16, :] = silu(jnp.concatenate([dz_ref[t].astype(F32) for t in range(STEPS)], 0))


def project_kernel(
    tails_ref, main_ref, cin_ref, x_ref, dx_ref, small_ref, xw_ref, part_ref, all_ref
):
    rows, width = cin_ref.shape
    taps = tails_ref.shape[1] + 1
    place = lax.axis_index("group")
    position = lax.rem(place, BLOCKS)
    bias = small_ref[2:3, :]
    w = small_ref[4 : 4 + taps, :]
    before = tails_ref[jnp.maximum(place - 1, 0)].astype(F32)
    before = jnp.where(position == 0, jnp.zeros_like(before), before)
    near = jnp.concatenate([before, x_ref[0:16, :].astype(F32)[0 : taps - 1]], 0)
    rim = bias
    for k in range(taps):
        rim = rim + w[k : k + 1] * near[k : k + taps - 1]
    first = tails_ref[BLOCKS - 1].astype(F32)
    second = tails_ref[2 * BLOCKS - 1].astype(F32)
    picked = [jnp.where(small_ref[16 + s : 17 + s, :] < 0.5, first, second) for s in range(2)]
    window = [
        jnp.concatenate([picked[0][k : k + 1], picked[1][k : k + 1]], 0) for k in range(taps - 1)
    ] + [dx_ref[t].astype(F32) for t in range(STEPS)]
    lines = []
    for t in range(STEPS):
        mixed = bias
        for k in range(taps):
            mixed = mixed + w[k : k + 1] * window[t + k]
        lines.append(mixed)
    extra = silu(jnp.concatenate([rim, jnp.zeros((8 - (taps - 1), width), F32)] + lines, 0))
    row = lax.broadcasted_iota(jnp.int32, (16, 1), 0)
    start = jnp.where(row < taps - 1, extra, cin_ref[0:16, :].astype(F32))
    all_ref[0:16, :] = start.astype(BF16)
    all_ref[16:rows, :] = cin_ref[16:rows, :]
    all_ref[rows : rows + 16, :] = jnp.concatenate(
        [extra[8:16], jnp.zeros((8, width), F32)], 0
    ).astype(BF16)
    extra = onto(extra.astype(BF16), xw_ref)
    extra = jnp.concatenate([extra, jnp.zeros((16, WIDE - R - 2 * N), F32)], 1)
    for k in range(part_ref.shape[0]):
        mine = main_ref[16 * k : 16 * k + 16, :]
        if k == 0:
            mine = jnp.where(row < taps - 1, extra, mine)
        part_ref[k, :, :R] = mine[:, :R].astype(BF16)
        part_ref[k, :, R:] = folded(mine[:, R:], extra[8 + k : 9 + k]).astype(BF16)


def near_sum_kernel(got_ref, out_ref):
    total = got_ref[0].astype(F32)
    for k in range(1, got_ref.shape[0]):
        total = total + got_ref[k].astype(F32)
    total = total.astype(BF16)
    for k in range(out_ref.shape[0]):
        out_ref[k] = total


def far_sum_kernel(got_ref, out_ref):
    total = (got_ref[0].astype(F32) + got_ref[1].astype(F32)) + (
        got_ref[2].astype(F32) + got_ref[3].astype(F32)
    )
    low = total[:, :R].astype(BF16)
    tile = with_rest(total[:, R:]).astype(BF16)
    for k in range(out_ref.shape[0]):
        out_ref[k, :, :R] = low
        out_ref[k, :, R:] = tile


def parts(value):
    head = value.astype(BF16)
    return head, (value - head.astype(F32)).astype(BF16)


def step_kernel(
    all_ref, cin_ref, dtw_ref, small_ref, nrate_ref,
    msg_ref, step_ref, bc_ref, u_ref, dbc_ref, low_ref, left_ref,
):
    rows, width = u_ref.shape
    lines, tiles = [], []
    for k in range(NEAR):
        at = slice(16 * k, 16 * k + 16)
        tile = all_ref[k, :, R:].astype(F32)
        low_ref[at, :] = all_ref[k, :, :R]
        bc_ref[at, :] = joined(tile)
        line, tile = unfolded(tile)
        lines.append(line)
        tiles.append(tile)
    low_ref[rows : rows + 16, :] = jnp.concatenate(
        lines + [jnp.zeros((8, width), F32)], 0
    ).astype(BF16)
    dbc_ref[...] = joined(jnp.concatenate(tiles, 0))
    step = softplus(
        jnp.dot(low_ref[...], dtw_ref[...], preferred_element_type=F32) + small_ref[0:1, :]
    )
    step_ref[...] = step
    step = step[:rows]
    u_ref[...] = step * cin_ref[0:rows, :].astype(F32)
    down = lax.broadcasted_iota(jnp.int32, (rows, rows), 0)
    over = lax.broadcasted_iota(jnp.int32, (rows, rows), 1)
    after = jnp.where(over > down, 1.0, 0.0).astype(BF16)
    left = sum(jnp.dot(after, part, preferred_element_type=F32) for part in parts(step))
    left_ref[...] = left
    ends = []
    for n in range(N):
        rate = nrate_ref[n : n + 1, :]
        acc = jnp.zeros((16, width), F32)
        for g in range(rows // 16):
            at = slice(16 * g, 16 * g + 16)
            acc = acc + jnp.exp(rate * left_ref[at, :]) * (bc_ref[at, n : n + 1] * u_ref[at, :])
        ends.append(jnp.sum(acc, axis=0, keepdims=True))
    total = left[0:1] + step[0:1]
    coarse = jnp.concatenate([total[:, 128 * k : 128 * k + 128] for k in range(width // 128)], 0)
    fine = coarse - coarse.astype(BF16).astype(F32)
    side = jnp.concatenate([coarse, fine, jnp.zeros((8, 128), F32)], 0)
    result = jnp.concatenate([jnp.concatenate(ends, 0), side], 1).astype(BF16)
    for k in range(msg_ref.shape[0]):
        msg_ref[k] = result


def scan_kernel(
    step_ref, u_ref, bc_ref, cin_ref, gate_ref, small_ref, nrate_ref, dbc_ref,
    out_ref, reach_ref, from_ref, dout_ref,
):
    rows, width = u_ref.shape
    down = lax.broadcasted_iota(jnp.int32, (rows, rows), 0)
    over = lax.broadcasted_iota(jnp.int32, (rows, rows), 1)
    upto = jnp.where(over <= down, 1.0, 0.0).astype(BF16)
    reach_ref[...] = sum(
        jnp.dot(upto, part, preferred_element_type=F32) for part in parts(step_ref[0:rows, :])
    )
    dbc = jnp.transpose(jnp.concatenate([dbc_ref[...], jnp.zeros((120, 128), F32)], 0))
    nrate = nrate_ref[...]
    skip = small_ref[1:2, :]
    bct = jnp.transpose(bc_ref[...])[0 : 2 * N]

    def group(g, carry):
        h, bc = carry
        at = pl.ds(pl.multiple_of(8 * g, 8), 8)
        d8 = step_ref[at, :]
        u8 = u_ref[at, :]
        values = []
        for j in range(8):
            h = jnp.exp(nrate * d8[j : j + 1]) * h + bc[0:N, j : j + 1] * u8[j : j + 1]
            values.append(jnp.sum(bc[N : 2 * N, j : j + 1] * h, axis=0, keepdims=True))
        out_ref[at, :] = jnp.concatenate(values, 0)
        return h, pltpu.roll(bc, 120, 1)

    lax.fori_loop(0, rows // 8, group, (jnp.zeros((N, width), F32), bct))
    out_ref[...] = (out_ref[...] + skip * cin_ref[0:rows, :].astype(F32)) * gate_ref[...]
    dec = cin_ref[rows : rows + 16, :].astype(F32)
    own = []
    kept = [jnp.ones((N, width), F32) for _ in range(2)]
    state = [jnp.zeros((N, width), F32) for _ in range(2)]
    for r in range(2 * STEPS):
        s = r % 2
        d = step_ref[rows + r : rows + r + 1, :]
        decay = jnp.exp(nrate * d)
        kept[s] = decay * kept[s]
        state[s] = decay * state[s] + dbc[0:N, r : r + 1] * (d * dec[r : r + 1])
        c = dbc[N : 2 * N, r : r + 1]
        from_ref[r] = c * kept[s]
        own.append(jnp.sum(c * state[s], axis=0, keepdims=True))
    dout_ref[...] = jnp.concatenate(own, 0) + skip * dec[0 : 2 * STEPS]


def finish_kernel(
    got_ref, y_ref, reach_ref, bc_ref, gate_ref, nrate_ref, small_ref, from_ref, own_ref,
    out_ref, dec_ref, in_ref,
):
    rows, width = y_ref.shape
    place = lax.axis_index("group")
    mine, position = lax.div(place, BLOCKS), lax.rem(place, BLOCKS)
    nrate = nrate_ref[...]
    finals = []
    incoming = jnp.zeros((N, width), F32)
    for p in range(2):
        h = jnp.zeros((N, width), F32)
        for k in range(BLOCKS):
            r = p * BLOCKS + k
            if k > 0:
                incoming = jnp.where((mine == p) & (position == k), h, incoming)
            side = got_ref[r, :, width:].astype(F32)
            total = side[0:4] + side[4:8]
            total = jnp.concatenate([total[i : i + 1] for i in range(4)], 1)
            h = jnp.exp(nrate * total) * h + got_ref[r, :, :width].astype(F32)
        finals.append(h)
    in_ref[...] = incoming

    def group(g, carry):
        at = pl.ds(pl.multiple_of(16 * g, 16), 16)
        s = reach_ref[at, :]
        c = bc_ref[at, :]
        acc = jnp.zeros((16, width), F32)
        for n in range(N):
            acc = acc + c[:, N + n : N + n + 1] * (
                in_ref[n : n + 1, :] * jnp.exp(nrate_ref[n : n + 1, :] * s)
            )
        out_ref[at, :] = (y_ref[at, :] + acc * gate_ref[at, :]).astype(BF16)
        return carry

    lax.fori_loop(0, rows // 16, group, 0)
    states = [
        jnp.where(small_ref[16 + s : 17 + s, :] < 0.5, finals[0], finals[1]) for s in range(2)
    ]
    for t in range(STEPS):
        pair = [
            jnp.sum(from_ref[2 * t + s] * states[s], axis=0, keepdims=True) for s in range(2)
        ]
        at = slice(2 * t, 2 * t + 2)
        value = (jnp.concatenate(pair, 0) + own_ref[at, :]) * small_ref[8 + 2 * t : 10 + 2 * t, :]
        dec_ref[t] = value.astype(BF16)


def call(kernel, outs, scratch=(), smem=0, hbm=0, inputs=0, name=None):
    vmem = pl.BlockSpec(memory_space=pltpu.VMEM)
    return pl.pallas_call(
        kernel,
        out_shape=outs,
        in_specs=[pl.BlockSpec(memory_space=pltpu.SMEM)] * smem
        + [pl.BlockSpec(memory_space=pl.ANY)] * hbm
        + [vmem] * inputs,
        out_specs=jax.tree.map(lambda _: vmem, outs),
        scratch_shapes=list(scratch),
        compiler_params=pltpu.CompilerParams(vmem_limit_bytes=24 * 1024 * 1024),
        name=name,
    )


def shape(*dims, kind=F32):
    return jax.ShapeDtypeStruct(dims, kind)


def local(
    x_prompt,
    z_prompt,
    conv_weight,
    conv_bias,
    xproj_weight,
    dtproj_weight,
    dt_bias,
    decay_rate,
    skip_gain,
    sample_prompt,
    decode_x,
    decode_z,
):
    rows, width = x_prompt.shape
    taps = conv_weight.shape[0]
    places = lax.axis_size("group")
    ring = lax.axis_size("tensor")
    deep = NEAR // 2
    near = [
        [NEAR * a + 2 * ((j + a) % deep) + y for j in range(deep) for y in range(2)]
        for a in range(ring // NEAR)
    ]
    far = [[g[j] for g in near] for j in range(NEAR)]

    tail = x_prompt[rows - (taps - 1) :]
    tails = lax.all_to_all(
        jnp.broadcast_to(tail[None], (places, taps - 1, width)), "group", 0, 0
    )
    columns = xproj_weight.T
    main, cin, nrate, gate, small = call(
        prepare_kernel,
        (
            shape(rows, WIDE),
            shape(rows, width, kind=BF16),
            shape(N, width),
            shape(rows, width),
            shape(24, width),
        ),
        [pltpu.VMEM((rows + 8, width), F32)],
        smem=1,
        inputs=9,
        name="prepare",
    )(
        sample_prompt,
        x_prompt,
        conv_weight,
        conv_bias,
        columns,
        decay_rate.T,
        z_prompt,
        decode_z,
        dt_bias,
        skip_gain,
    )
    part, cin = call(
        project_kernel,
        (shape(NEAR, 16, WIDE, kind=BF16), shape(rows + 16, width, kind=BF16)),
        inputs=7,
        name="project",
    )(tails, main, cin, x_prompt, decode_x, small, columns)

    got = lax.all_to_all(part, "tensor", 0, 0, axis_index_groups=near)
    sums = call(
        near_sum_kernel, shape(ring // NEAR, 16, WIDE, kind=BF16), inputs=1, name="near_sum"
    )(got)
    got = lax.all_to_all(sums, "tensor", 0, 0, axis_index_groups=far)
    sums = call(far_sum_kernel, shape(NEAR, 16, WIDE, kind=BF16), inputs=1, name="far_sum")(got)
    everything = lax.all_to_all(sums, "tensor", 0, 0, axis_index_groups=near)

    send, step, bc, u, dbc = call(
        step_kernel,
        (
            shape(places, N, width + 128, kind=BF16),
            shape(rows + 16, width),
            shape(rows, 128),
            shape(rows, width),
            shape(8, 128),
        ),
        [pltpu.VMEM((rows + 16, R), BF16), pltpu.VMEM((rows, width), F32)],
        inputs=5,
        name="step",
    )(everything, cin, dtproj_weight, small, nrate)
    states = lax.all_to_all(send, "group", 0, 0)
    y, reach, share, own = call(
        scan_kernel,
        (
            shape(rows, width),
            shape(rows, width),
            shape(2 * STEPS, N, width),
            shape(2 * STEPS, width),
        ),
        inputs=8,
        name="scan",
    )(step, u, bc, cin, gate, small, nrate, dbc)
    return call(
        finish_kernel,
        (shape(rows, width, kind=BF16), shape(STEPS, 2, width, kind=BF16)),
        [pltpu.VMEM((N, width), F32)],
        inputs=9,
        name="finish",
    )(states, y, reach, bc, gate, nrate, small, share, own)


def solution(mesh):
    placed = (
        P("group", "tensor"),
        P("group", "tensor"),
        P(None, "tensor"),
        P("tensor"),
        P("tensor", None),
        P(None, "tensor"),
        P("tensor"),
        P("tensor", None),
        P("tensor"),
        P("group"),
        P(None, "group", "tensor"),
        P(None, "group", "tensor"),
    )
    return jax.shard_map(
        local,
        mesh=mesh,
        in_specs=placed,
        out_specs=(P("group", "tensor"), P(None, "group", "tensor")),
        check_vma=False,
    )
```

```python
import jax
import jax.numpy as jnp
from jax import lax
from jax.experimental import pallas as pl
from jax.experimental.pallas import tpu as pltpu
from jax.sharding import PartitionSpec as P

N = 16
R = 512
STEPS = 4
F32 = jnp.float32
BF16 = jnp.bfloat16
WIDE = 640
BLOCKS = 8
NEAR = 8


def silu(v):
    return v * jax.nn.sigmoid(v)


def softplus(v):
    return jnp.maximum(v, 0.0) + jnp.log1p(jnp.exp(-jnp.abs(v)))


def folded(tile, line):
    lane = lax.broadcasted_iota(jnp.int32, tile.shape, 1)
    four = jnp.concatenate([line[:, 128 * i : 128 * i + 128] for i in range(4)], 0)
    last = pltpu.roll(line[:, R:], 64, 1)
    side = jnp.concatenate([pltpu.roll(four, 64, 1), four, last, jnp.zeros((7, 128), F32)], 0)
    return jnp.where(lane < 64, tile, side)


def unfolded(tile):
    lane = lax.broadcasted_iota(jnp.int32, (4, 128), 1)
    four = jnp.where(lane < 64, pltpu.roll(tile[0:4], 64, 1), tile[4:8])
    return jnp.concatenate([four[i : i + 1] for i in range(4)], 1), pltpu.roll(tile[8:9], 64, 1)


def with_rest(tile):
    lane = lax.broadcasted_iota(jnp.int32, tile.shape, 1)
    row = lax.broadcasted_iota(jnp.int32, tile.shape, 0)
    head = tile.astype(BF16).astype(F32)
    rest = pltpu.roll(tile - head, 2 * N, 1)
    plain = (lax.rem(lane, 64) < 2 * N) | ((lane >= 64) & (row < 8))
    return jnp.where(plain, head, rest)


def joined(block):
    return block + pltpu.roll(block, 128 - 2 * N, 1)


def onto(rows, columns_ref):
    return lax.dot_general(
        rows, columns_ref[...], (((1,), (1,)), ((), ())), preferred_element_type=F32
    )


def prepare_kernel(
    sp_ref, x_ref, w_ref, b_ref, xw_ref, rate_ref, z_ref, dz_ref, db_ref, skip_ref,
    part_ref, cin_ref, nrate_ref, gate_ref, small_ref, ext,
):
    rows, width = x_ref.shape
    ext[0:8, :] = jnp.zeros((8, width), F32)
    ext[8 : 8 + rows, :] = x_ref[...].astype(F32)
    w = w_ref[...].astype(F32)
    taps = w.shape[0]
    bias = b_ref[...].astype(F32).reshape(1, width)
    mixed = bias
    for k in range(taps):
        mixed = mixed + w[k : k + 1] * ext[9 - taps + k : 9 - taps + k + rows, :]
    cin = silu(mixed).astype(BF16)
    cin_ref[...] = cin
    part_ref[:, : R + 2 * N] = onto(cin, xw_ref)
    part_ref[:, R + 2 * N :] = jnp.zeros((rows, WIDE - R - 2 * N), F32)
    nrate_ref[...] = -rate_ref[...]
    gate_ref[...] = silu(z_ref[...].astype(F32))
    small_ref[0:8, :] = jnp.concatenate(
        [
            db_ref[...].reshape(1, width),
            skip_ref[...].reshape(1, width),
            bias,
            jnp.zeros((1, width), F32),
            w,
        ],
        0,
    )
    for s in range(2):
        small_ref[16 + s : 17 + s, :] = jnp.full((1, width), sp_ref[s], jnp.int32).astype(F32)
    small_ref[8:16, :] = silu(jnp.concatenate([dz_ref[t].astype(F32) for t in range(STEPS)], 0))


def project_kernel(
    tails_ref, main_ref, cin_ref, x_ref, dx_ref, small_ref, xw_ref, part_ref, all_ref
):
    rows, width = cin_ref.shape
    taps = tails_ref.shape[1] + 1
    place = lax.axis_index("group")
    position = lax.rem(place, BLOCKS)
    bias = small_ref[2:3, :]
    w = small_ref[4 : 4 + taps, :]
    before = tails_ref[jnp.maximum(place - 1, 0)].astype(F32)
    before = jnp.where(position == 0, jnp.zeros_like(before), before)
    near = jnp.concatenate([before, x_ref[0:16, :].astype(F32)[0 : taps - 1]], 0)
    rim = bias
    for k in range(taps):
        rim = rim + w[k : k + 1] * near[k : k + taps - 1]
    first = tails_ref[BLOCKS - 1].astype(F32)
    second = tails_ref[2 * BLOCKS - 1].astype(F32)
    picked = [jnp.where(small_ref[16 + s : 17 + s, :] < 0.5, first, second) for s in range(2)]
    window = [
        jnp.concatenate([picked[0][k : k + 1], picked[1][k : k + 1]], 0) for k in range(taps - 1)
    ] + [dx_ref[t].astype(F32) for t in range(STEPS)]
    lines = []
    for t in range(STEPS):
        mixed = bias
        for k in range(taps):
            mixed = mixed + w[k : k + 1] * window[t + k]
        lines.append(mixed)
    extra = silu(jnp.concatenate([rim, jnp.zeros((8 - (taps - 1), width), F32)] + lines, 0))
    row = lax.broadcasted_iota(jnp.int32, (16, 1), 0)
    start = jnp.where(row < taps - 1, extra, cin_ref[0:16, :].astype(F32))
    all_ref[0:16, :] = start.astype(BF16)
    all_ref[16:rows, :] = cin_ref[16:rows, :]
    all_ref[rows : rows + 16, :] = jnp.concatenate(
        [extra[8:16], jnp.zeros((8, width), F32)], 0
    ).astype(BF16)
    extra = onto(extra.astype(BF16), xw_ref)
    extra = jnp.concatenate([extra, jnp.zeros((16, WIDE - R - 2 * N), F32)], 1)
    for k in range(part_ref.shape[0]):
        mine = main_ref[16 * k : 16 * k + 16, :]
        if k == 0:
            mine = jnp.where(row < taps - 1, extra, mine)
        part_ref[k, :, :R] = mine[:, :R].astype(BF16)
        part_ref[k, :, R:] = folded(mine[:, R:], extra[8 + k : 9 + k]).astype(BF16)


def near_sum_kernel(got_ref, out_ref):
    total = got_ref[0].astype(F32)
    for k in range(1, got_ref.shape[0]):
        total = total + got_ref[k].astype(F32)
    total = total.astype(BF16)
    for k in range(out_ref.shape[0]):
        out_ref[k] = total


def far_sum_kernel(got_ref, out_ref):
    total = (got_ref[0].astype(F32) + got_ref[1].astype(F32)) + (
        got_ref[2].astype(F32) + got_ref[3].astype(F32)
    )
    low = total[:, :R].astype(BF16)
    tile = with_rest(total[:, R:]).astype(BF16)
    for k in range(out_ref.shape[0]):
        out_ref[k, :, :R] = low
        out_ref[k, :, R:] = tile


def parts(value):
    head = value.astype(BF16)
    return head, (value - head.astype(F32)).astype(BF16)


def step_kernel(
    all_ref, cin_ref, dtw_ref, small_ref, nrate_ref,
    msg_ref, step_ref, bc_ref, u_ref, dbc_ref, low_ref, left_ref,
):
    rows, width = u_ref.shape
    lines, tiles = [], []
    for k in range(NEAR):
        at = slice(16 * k, 16 * k + 16)
        tile = all_ref[k, :, R:].astype(F32)
        low_ref[at, :] = all_ref[k, :, :R]
        bc_ref[at, :] = joined(tile)
        line, tile = unfolded(tile)
        lines.append(line)
        tiles.append(tile)
    low_ref[rows : rows + 16, :] = jnp.concatenate(
        lines + [jnp.zeros((8, width), F32)], 0
    ).astype(BF16)
    dbc_ref[...] = joined(jnp.concatenate(tiles, 0))
    step = softplus(
        jnp.dot(low_ref[...], dtw_ref[...], preferred_element_type=F32) + small_ref[0:1, :]
    )
    step_ref[...] = step
    step = step[:rows]
    u_ref[...] = step * cin_ref[0:rows, :].astype(F32)
    down = lax.broadcasted_iota(jnp.int32, (rows, rows), 0)
    over = lax.broadcasted_iota(jnp.int32, (rows, rows), 1)
    after = jnp.where(over > down, 1.0, 0.0).astype(BF16)
    left = sum(jnp.dot(after, part, preferred_element_type=F32) for part in parts(step))
    left_ref[...] = left
    ends = []
    for n in range(N):
        rate = nrate_ref[n : n + 1, :]
        acc = jnp.zeros((16, width), F32)
        for g in range(rows // 16):
            at = slice(16 * g, 16 * g + 16)
            acc = acc + jnp.exp(rate * left_ref[at, :]) * (bc_ref[at, n : n + 1] * u_ref[at, :])
        ends.append(jnp.sum(acc, axis=0, keepdims=True))
    total = left[0:1] + step[0:1]
    coarse = jnp.concatenate([total[:, 128 * k : 128 * k + 128] for k in range(width // 128)], 0)
    fine = coarse - coarse.astype(BF16).astype(F32)
    ends = jnp.concatenate(ends, 0)
    side = jnp.concatenate([coarse, fine], 0)
    result = jnp.concatenate([ends[:8], ends[8:], side], 1).astype(BF16)
    for k in range(msg_ref.shape[0]):
        msg_ref[k] = result


def scan_kernel(
    step_ref, u_ref, bc_ref, cin_ref, gate_ref, small_ref, nrate_ref, dbc_ref,
    out_ref, reach_ref, from_ref, dout_ref,
):
    rows, width = u_ref.shape
    down = lax.broadcasted_iota(jnp.int32, (rows, rows), 0)
    over = lax.broadcasted_iota(jnp.int32, (rows, rows), 1)
    upto = jnp.where(over <= down, 1.0, 0.0).astype(BF16)
    reach_ref[...] = sum(
        jnp.dot(upto, part, preferred_element_type=F32) for part in parts(step_ref[0:rows, :])
    )
    dbc = jnp.transpose(jnp.concatenate([dbc_ref[...], jnp.zeros((120, 128), F32)], 0))
    nrate = nrate_ref[...]
    skip = small_ref[1:2, :]
    bct = jnp.transpose(bc_ref[...])[0 : 2 * N]

    def group(g, carry):
        h, bc = carry
        at = pl.ds(pl.multiple_of(8 * g, 8), 8)
        d8 = step_ref[at, :]
        u8 = u_ref[at, :]
        values = []
        for j in range(8):
            h = jnp.exp(nrate * d8[j : j + 1]) * h + bc[0:N, j : j + 1] * u8[j : j + 1]
            values.append(jnp.sum(bc[N : 2 * N, j : j + 1] * h, axis=0, keepdims=True))
        out_ref[at, :] = jnp.concatenate(values, 0)
        return h, pltpu.roll(bc, 120, 1)

    lax.fori_loop(0, rows // 8, group, (jnp.zeros((N, width), F32), bct))
    out_ref[...] = (out_ref[...] + skip * cin_ref[0:rows, :].astype(F32)) * gate_ref[...]
    dec = cin_ref[rows : rows + 16, :].astype(F32)
    own = []
    kept = [jnp.ones((N, width), F32) for _ in range(2)]
    state = [jnp.zeros((N, width), F32) for _ in range(2)]
    for r in range(2 * STEPS):
        s = r % 2
        d = step_ref[rows + r : rows + r + 1, :]
        decay = jnp.exp(nrate * d)
        kept[s] = decay * kept[s]
        state[s] = decay * state[s] + dbc[0:N, r : r + 1] * (d * dec[r : r + 1])
        c = dbc[N : 2 * N, r : r + 1]
        from_ref[r] = c * kept[s]
        own.append(jnp.sum(c * state[s], axis=0, keepdims=True))
    dout_ref[...] = jnp.concatenate(own, 0) + skip * dec[0 : 2 * STEPS]


def finish_kernel(
    got_ref, y_ref, reach_ref, bc_ref, gate_ref, nrate_ref, small_ref, from_ref, own_ref,
    out_ref, dec_ref, in_ref,
):
    rows, width = y_ref.shape
    place = lax.axis_index("group")
    mine, position = lax.div(place, BLOCKS), lax.rem(place, BLOCKS)
    nrate = nrate_ref[...]
    finals = []
    incoming = jnp.zeros((N, width), F32)
    for p in range(2):
        h = jnp.zeros((N, width), F32)
        for k in range(BLOCKS):
            r = p * BLOCKS + k
            if k > 0:
                incoming = jnp.where((mine == p) & (position == k), h, incoming)
            block = got_ref[r].astype(F32)
            side = block[:, 2 * width :]
            total = side[0:4] + side[4:8]
            total = jnp.concatenate([total[i : i + 1] for i in range(4)], 1)
            end = jnp.concatenate([block[:, :width], block[:, width : 2 * width]], 0)
            h = jnp.exp(nrate * total) * h + end
        finals.append(h)
    in_ref[...] = incoming

    def group(g, carry):
        at = pl.ds(pl.multiple_of(16 * g, 16), 16)
        s = reach_ref[at, :]
        c = bc_ref[at, :]
        acc = jnp.zeros((16, width), F32)
        for n in range(N):
            acc = acc + c[:, N + n : N + n + 1] * (
                in_ref[n : n + 1, :] * jnp.exp(nrate_ref[n : n + 1, :] * s)
            )
        out_ref[at, :] = (y_ref[at, :] + acc * gate_ref[at, :]).astype(BF16)
        return carry

    lax.fori_loop(0, rows // 16, group, 0)
    states = [
        jnp.where(small_ref[16 + s : 17 + s, :] < 0.5, finals[0], finals[1]) for s in range(2)
    ]
    for t in range(STEPS):
        pair = [
            jnp.sum(from_ref[2 * t + s] * states[s], axis=0, keepdims=True) for s in range(2)
        ]
        at = slice(2 * t, 2 * t + 2)
        value = (jnp.concatenate(pair, 0) + own_ref[at, :]) * small_ref[8 + 2 * t : 10 + 2 * t, :]
        dec_ref[t] = value.astype(BF16)


def call(kernel, outs, scratch=(), smem=0, hbm=0, inputs=0, name=None):
    vmem = pl.BlockSpec(memory_space=pltpu.VMEM)
    return pl.pallas_call(
        kernel,
        out_shape=outs,
        in_specs=[pl.BlockSpec(memory_space=pltpu.SMEM)] * smem
        + [pl.BlockSpec(memory_space=pl.ANY)] * hbm
        + [vmem] * inputs,
        out_specs=jax.tree.map(lambda _: vmem, outs),
        scratch_shapes=list(scratch),
        compiler_params=pltpu.CompilerParams(vmem_limit_bytes=24 * 1024 * 1024),
        name=name,
    )


def shape(*dims, kind=F32):
    return jax.ShapeDtypeStruct(dims, kind)


def local(
    x_prompt,
    z_prompt,
    conv_weight,
    conv_bias,
    xproj_weight,
    dtproj_weight,
    dt_bias,
    decay_rate,
    skip_gain,
    sample_prompt,
    decode_x,
    decode_z,
):
    rows, width = x_prompt.shape
    taps = conv_weight.shape[0]
    places = lax.axis_size("group")
    ring = lax.axis_size("tensor")
    deep = NEAR // 2
    near = [
        [NEAR * a + 2 * ((j + a) % deep) + y for j in range(deep) for y in range(2)]
        for a in range(ring // NEAR)
    ]
    far = [[g[j] for g in near] for j in range(NEAR)]

    tail = x_prompt[rows - (taps - 1) :]
    tails = lax.all_to_all(
        jnp.broadcast_to(tail[None], (places, taps - 1, width)), "group", 0, 0
    )
    columns = xproj_weight.T
    main, cin, nrate, gate, small = call(
        prepare_kernel,
        (
            shape(rows, WIDE),
            shape(rows, width, kind=BF16),
            shape(N, width),
            shape(rows, width),
            shape(24, width),
        ),
        [pltpu.VMEM((rows + 8, width), F32)],
        smem=1,
        inputs=9,
        name="prepare",
    )(
        sample_prompt,
        x_prompt,
        conv_weight,
        conv_bias,
        columns,
        decay_rate.T,
        z_prompt,
        decode_z,
        dt_bias,
        skip_gain,
    )
    part, cin = call(
        project_kernel,
        (shape(NEAR, 16, WIDE, kind=BF16), shape(rows + 16, width, kind=BF16)),
        inputs=7,
        name="project",
    )(tails, main, cin, x_prompt, decode_x, small, columns)

    got = lax.all_to_all(part, "tensor", 0, 0, axis_index_groups=near)
    sums = call(
        near_sum_kernel, shape(ring // NEAR, 16, WIDE, kind=BF16), inputs=1, name="near_sum"
    )(got)
    got = lax.all_to_all(sums, "tensor", 0, 0, axis_index_groups=far)
    sums = call(far_sum_kernel, shape(NEAR, 16, WIDE, kind=BF16), inputs=1, name="far_sum")(got)
    everything = lax.all_to_all(sums, "tensor", 0, 0, axis_index_groups=near)

    send, step, bc, u, dbc = call(
        step_kernel,
        (
            shape(places, N // 2, 2 * width + 128, kind=BF16),
            shape(rows + 16, width),
            shape(rows, 128),
            shape(rows, width),
            shape(8, 128),
        ),
        [pltpu.VMEM((rows + 16, R), BF16), pltpu.VMEM((rows, width), F32)],
        inputs=5,
        name="step",
    )(everything, cin, dtproj_weight, small, nrate)
    states = lax.all_to_all(send, "group", 0, 0)
    y, reach, share, own = call(
        scan_kernel,
        (
            shape(rows, width),
            shape(rows, width),
            shape(2 * STEPS, N, width),
            shape(2 * STEPS, width),
        ),
        inputs=8,
        name="scan",
    )(step, u, bc, cin, gate, small, nrate, dbc)
    return call(
        finish_kernel,
        (shape(rows, width, kind=BF16), shape(STEPS, 2, width, kind=BF16)),
        [pltpu.VMEM((N, width), F32)],
        inputs=9,
        name="finish",
    )(states, y, reach, bc, gate, nrate, small, share, own)


def solution(mesh):
    placed = (
        P("group", "tensor"),
        P("group", "tensor"),
        P(None, "tensor"),
        P("tensor"),
        P("tensor", None),
        P(None, "tensor"),
        P("tensor"),
        P("tensor", None),
        P("tensor"),
        P("group"),
        P(None, "group", "tensor"),
        P(None, "group", "tensor"),
    )
    return jax.shard_map(
        local,
        mesh=mesh,
        in_specs=placed,
        out_specs=(P("group", "tensor"), P(None, "group", "tensor")),
        check_vma=False,
    )
```

```python
import jax
import jax.numpy as jnp
from jax import lax
from jax.experimental import pallas as pl
from jax.experimental.pallas import tpu as pltpu
from jax.sharding import PartitionSpec as P

N = 16
KEPT = 8
R = 512
STEPS = 4
F32 = jnp.float32
BF16 = jnp.bfloat16
WIDE = 640
BLOCKS = 8
NEAR = 8


def silu(v):
    return v * jax.nn.sigmoid(v)


def softplus(v):
    return jnp.maximum(v, 0.0) + jnp.log1p(jnp.exp(-jnp.abs(v)))


def folded(tile, line):
    lane = lax.broadcasted_iota(jnp.int32, tile.shape, 1)
    four = jnp.concatenate([line[:, 128 * i : 128 * i + 128] for i in range(4)], 0)
    last = pltpu.roll(line[:, R:], 64, 1)
    side = jnp.concatenate([pltpu.roll(four, 64, 1), four, last, jnp.zeros((7, 128), F32)], 0)
    return jnp.where(lane < 64, tile, side)


def unfolded(tile):
    lane = lax.broadcasted_iota(jnp.int32, (4, 128), 1)
    four = jnp.where(lane < 64, pltpu.roll(tile[0:4], 64, 1), tile[4:8])
    return jnp.concatenate([four[i : i + 1] for i in range(4)], 1), pltpu.roll(tile[8:9], 64, 1)


def with_rest(tile):
    lane = lax.broadcasted_iota(jnp.int32, tile.shape, 1)
    row = lax.broadcasted_iota(jnp.int32, tile.shape, 0)
    head = tile.astype(BF16).astype(F32)
    rest = pltpu.roll(tile - head, 2 * N, 1)
    plain = (lax.rem(lane, 64) < 2 * N) | ((lane >= 64) & (row < 8))
    return jnp.where(plain, head, rest)


def joined(block):
    return block + pltpu.roll(block, 128 - 2 * N, 1)


def onto(rows, columns_ref):
    return lax.dot_general(
        rows, columns_ref[...], (((1,), (1,)), ((), ())), preferred_element_type=F32
    )


def prepare_kernel(
    sp_ref, x_ref, w_ref, b_ref, xw_ref, rate_ref, z_ref, dz_ref, db_ref, skip_ref,
    part_ref, cin_ref, nrate_ref, gate_ref, small_ref, ext,
):
    rows, width = x_ref.shape
    ext[0:8, :] = jnp.zeros((8, width), F32)
    ext[8 : 8 + rows, :] = x_ref[...].astype(F32)
    w = w_ref[...].astype(F32)
    taps = w.shape[0]
    bias = b_ref[...].astype(F32).reshape(1, width)
    mixed = bias
    for k in range(taps):
        mixed = mixed + w[k : k + 1] * ext[9 - taps + k : 9 - taps + k + rows, :]
    cin = silu(mixed).astype(BF16)
    cin_ref[...] = cin
    part_ref[:, : R + 2 * N] = onto(cin, xw_ref)
    part_ref[:, R + 2 * N :] = jnp.zeros((rows, WIDE - R - 2 * N), F32)
    nrate_ref[...] = -rate_ref[...]
    gate_ref[...] = silu(z_ref[...].astype(F32))
    small_ref[0:8, :] = jnp.concatenate(
        [
            db_ref[...].reshape(1, width),
            skip_ref[...].reshape(1, width),
            bias,
            jnp.zeros((1, width), F32),
            w,
        ],
        0,
    )
    for s in range(2):
        small_ref[16 + s : 17 + s, :] = jnp.full((1, width), sp_ref[s], jnp.int32).astype(F32)
    small_ref[8:16, :] = silu(jnp.concatenate([dz_ref[t].astype(F32) for t in range(STEPS)], 0))


def project_kernel(
    tails_ref, main_ref, cin_ref, x_ref, dx_ref, small_ref, xw_ref, part_ref, all_ref
):
    rows, width = cin_ref.shape
    taps = tails_ref.shape[1] + 1
    place = lax.axis_index("group")
    position = lax.rem(place, BLOCKS)
    bias = small_ref[2:3, :]
    w = small_ref[4 : 4 + taps, :]
    before = tails_ref[jnp.maximum(place - 1, 0)].astype(F32)
    before = jnp.where(position == 0, jnp.zeros_like(before), before)
    near = jnp.concatenate([before, x_ref[0:16, :].astype(F32)[0 : taps - 1]], 0)
    rim = bias
    for k in range(taps):
        rim = rim + w[k : k + 1] * near[k : k + taps - 1]
    first = tails_ref[BLOCKS - 1].astype(F32)
    second = tails_ref[2 * BLOCKS - 1].astype(F32)
    picked = [jnp.where(small_ref[16 + s : 17 + s, :] < 0.5, first, second) for s in range(2)]
    window = [
        jnp.concatenate([picked[0][k : k + 1], picked[1][k : k + 1]], 0) for k in range(taps - 1)
    ] + [dx_ref[t].astype(F32) for t in range(STEPS)]
    lines = []
    for t in range(STEPS):
        mixed = bias
        for k in range(taps):
            mixed = mixed + w[k : k + 1] * window[t + k]
        lines.append(mixed)
    extra = silu(jnp.concatenate([rim, jnp.zeros((8 - (taps - 1), width), F32)] + lines, 0))
    row = lax.broadcasted_iota(jnp.int32, (16, 1), 0)
    start = jnp.where(row < taps - 1, extra, cin_ref[0:16, :].astype(F32))
    all_ref[0:16, :] = start.astype(BF16)
    all_ref[16:rows, :] = cin_ref[16:rows, :]
    all_ref[rows : rows + 16, :] = jnp.concatenate(
        [extra[8:16], jnp.zeros((8, width), F32)], 0
    ).astype(BF16)
    extra = onto(extra.astype(BF16), xw_ref)
    extra = jnp.concatenate([extra, jnp.zeros((16, WIDE - R - 2 * N), F32)], 1)
    for k in range(part_ref.shape[0]):
        mine = main_ref[16 * k : 16 * k + 16, :]
        if k == 0:
            mine = jnp.where(row < taps - 1, extra, mine)
        part_ref[k, :, :R] = mine[:, :R].astype(BF16)
        part_ref[k, :, R:] = folded(mine[:, R:], extra[8 + k : 9 + k]).astype(BF16)


def near_sum_kernel(got_ref, out_ref):
    total = got_ref[0].astype(F32)
    for k in range(1, got_ref.shape[0]):
        total = total + got_ref[k].astype(F32)
    total = total.astype(BF16)
    for k in range(out_ref.shape[0]):
        out_ref[k] = total


def far_sum_kernel(got_ref, out_ref):
    total = (got_ref[0].astype(F32) + got_ref[1].astype(F32)) + (
        got_ref[2].astype(F32) + got_ref[3].astype(F32)
    )
    low = total[:, :R].astype(BF16)
    tile = with_rest(total[:, R:]).astype(BF16)
    for k in range(out_ref.shape[0]):
        out_ref[k, :, :R] = low
        out_ref[k, :, R:] = tile


def parts(value):
    head = value.astype(BF16)
    return head, (value - head.astype(F32)).astype(BF16)


def step_kernel(
    all_ref, cin_ref, dtw_ref, small_ref, nrate_ref,
    msg_ref, step_ref, bc_ref, dbc_ref, low_ref, left_ref, u_ref,
):
    rows, width = u_ref.shape
    lines, tiles = [], []
    for k in range(NEAR):
        at = slice(16 * k, 16 * k + 16)
        tile = all_ref[k, :, R:].astype(F32)
        low_ref[at, :] = all_ref[k, :, :R]
        bc_ref[at, :] = joined(tile)
        line, tile = unfolded(tile)
        lines.append(line)
        tiles.append(tile)
    low_ref[rows : rows + 16, :] = jnp.concatenate(
        lines + [jnp.zeros((8, width), F32)], 0
    ).astype(BF16)
    dbc_ref[...] = joined(jnp.concatenate(tiles, 0))
    step = softplus(
        jnp.dot(low_ref[...], dtw_ref[...], preferred_element_type=F32) + small_ref[0:1, :]
    )
    step_ref[...] = step
    step = step[:rows]
    u_ref[...] = step * cin_ref[0:rows, :].astype(F32)
    down = lax.broadcasted_iota(jnp.int32, (rows, rows), 0)
    over = lax.broadcasted_iota(jnp.int32, (rows, rows), 1)
    after = jnp.where(over > down, 1.0, 0.0).astype(BF16)
    left = sum(jnp.dot(after, part, preferred_element_type=F32) for part in parts(step))
    left_ref[...] = left
    ends = []
    for n in range(N):
        rate = nrate_ref[n : n + 1, :]
        acc = jnp.zeros((16, width), F32)
        for g in range(rows // 16):
            at = slice(16 * g, 16 * g + 16)
            acc = acc + jnp.exp(rate * left_ref[at, :]) * (bc_ref[at, n : n + 1] * u_ref[at, :])
        ends.append(jnp.sum(acc, axis=0, keepdims=True))
    total = left[0:1] + step[0:1]
    coarse = jnp.concatenate([total[:, 128 * k : 128 * k + 128] for k in range(width // 128)], 0)
    fine = coarse - coarse.astype(BF16).astype(F32)
    ends = jnp.concatenate(ends, 0)
    side = jnp.concatenate([coarse, fine], 0)
    result = jnp.concatenate([ends[:8], ends[8:], side], 1).astype(BF16)
    for k in range(msg_ref.shape[0]):
        msg_ref[k] = result


def scan_kernel(
    step_ref, bc_ref, cin_ref, gate_ref, small_ref, nrate_ref, dbc_ref,
    out_ref, reach_ref, carry_ref, from_ref, dout_ref, u_ref,
):
    rows, width = u_ref.shape
    down = lax.broadcasted_iota(jnp.int32, (rows, rows), 0)
    over = lax.broadcasted_iota(jnp.int32, (rows, rows), 1)
    u_ref[...] = step_ref[0:rows, :] * cin_ref[0:rows, :].astype(F32)
    upto = jnp.where(over <= down, 1.0, 0.0).astype(BF16)
    reach_ref[...] = sum(
        jnp.dot(upto, part, preferred_element_type=F32) for part in parts(step_ref[0:rows, :])
    )

    def carried(g, keep):
        at = pl.ds(pl.multiple_of(16 * g, 16), 16)
        reach = reach_ref[at, :]
        for n in range(KEPT):
            factor = jnp.exp(nrate_ref[n : n + 1, :] * reach)
            carry_ref[n, at, :] = (bc_ref[at, N + n : N + n + 1] * factor).astype(BF16)
        return keep

    lax.fori_loop(0, rows // 16, carried, 0)
    dbc = jnp.transpose(jnp.concatenate([dbc_ref[...], jnp.zeros((120, 128), F32)], 0))
    nrate = nrate_ref[...]
    skip = small_ref[1:2, :]
    bct = jnp.transpose(bc_ref[...])[0 : 2 * N]

    def group(g, carry):
        h, bc = carry
        at = pl.ds(pl.multiple_of(8 * g, 8), 8)
        d8 = step_ref[at, :]
        u8 = u_ref[at, :]
        values = []
        for j in range(8):
            h = jnp.exp(nrate * d8[j : j + 1]) * h + bc[0:N, j : j + 1] * u8[j : j + 1]
            values.append(jnp.sum(bc[N : 2 * N, j : j + 1] * h, axis=0, keepdims=True))
        out_ref[at, :] = jnp.concatenate(values, 0)
        return h, pltpu.roll(bc, 120, 1)

    lax.fori_loop(0, rows // 8, group, (jnp.zeros((N, width), F32), bct))
    out_ref[...] = (out_ref[...] + skip * cin_ref[0:rows, :].astype(F32)) * gate_ref[...]
    dec = cin_ref[rows : rows + 16, :].astype(F32)
    own = []
    kept = [jnp.ones((N, width), F32) for _ in range(2)]
    state = [jnp.zeros((N, width), F32) for _ in range(2)]
    for r in range(2 * STEPS):
        s = r % 2
        d = step_ref[rows + r : rows + r + 1, :]
        decay = jnp.exp(nrate * d)
        kept[s] = decay * kept[s]
        state[s] = decay * state[s] + dbc[0:N, r : r + 1] * (d * dec[r : r + 1])
        c = dbc[N : 2 * N, r : r + 1]
        from_ref[r] = (c * kept[s]).astype(BF16)
        own.append(jnp.sum(c * state[s], axis=0, keepdims=True))
    dout_ref[...] = jnp.concatenate(own, 0) + skip * dec[0 : 2 * STEPS]


def finish_kernel(
    got_ref, y_ref, reach_ref, carry_ref, bc_ref, gate_ref, nrate_ref, small_ref, from_ref, own_ref,
    out_ref, dec_ref, in_ref,
):
    rows, width = y_ref.shape
    place = lax.axis_index("group")
    mine, position = lax.div(place, BLOCKS), lax.rem(place, BLOCKS)
    nrate = nrate_ref[...]
    finals = []
    incoming = jnp.zeros((N, width), F32)
    for p in range(2):
        h = jnp.zeros((N, width), F32)
        for k in range(BLOCKS):
            r = p * BLOCKS + k
            if k > 0:
                incoming = jnp.where((mine == p) & (position == k), h, incoming)
            block = got_ref[r].astype(F32)
            side = block[:, 2 * width :]
            total = side[0:4] + side[4:8]
            total = jnp.concatenate([total[i : i + 1] for i in range(4)], 1)
            end = jnp.concatenate([block[:, :width], block[:, width : 2 * width]], 0)
            h = jnp.exp(nrate * total) * h + end
        finals.append(h)
    in_ref[...] = incoming

    def group(g, carry):
        at = pl.ds(pl.multiple_of(16 * g, 16), 16)
        s = reach_ref[at, :]
        c = bc_ref[at, :]
        acc = jnp.zeros((16, width), F32)
        for n in range(KEPT):
            acc = acc + in_ref[n : n + 1, :] * carry_ref[n, at, :].astype(F32)
        for n in range(KEPT, N):
            acc = acc + c[:, N + n : N + n + 1] * (
                in_ref[n : n + 1, :] * jnp.exp(nrate_ref[n : n + 1, :] * s)
            )
        out_ref[at, :] = (y_ref[at, :] + acc * gate_ref[at, :]).astype(BF16)
        return carry

    lax.fori_loop(0, rows // 16, group, 0)
    states = [
        jnp.where(small_ref[16 + s : 17 + s, :] < 0.5, finals[0], finals[1]) for s in range(2)
    ]
    for t in range(STEPS):
        pair = [
            jnp.sum(from_ref[2 * t + s].astype(F32) * states[s], axis=0, keepdims=True) for s in range(2)
        ]
        at = slice(2 * t, 2 * t + 2)
        value = (jnp.concatenate(pair, 0) + own_ref[at, :]) * small_ref[8 + 2 * t : 10 + 2 * t, :]
        dec_ref[t] = value.astype(BF16)


def call(kernel, outs, scratch=(), smem=0, hbm=0, inputs=0, name=None):
    vmem = pl.BlockSpec(memory_space=pltpu.VMEM)
    return pl.pallas_call(
        kernel,
        out_shape=outs,
        in_specs=[pl.BlockSpec(memory_space=pltpu.SMEM)] * smem
        + [pl.BlockSpec(memory_space=pl.ANY)] * hbm
        + [vmem] * inputs,
        out_specs=jax.tree.map(lambda _: vmem, outs),
        scratch_shapes=list(scratch),
        compiler_params=pltpu.CompilerParams(vmem_limit_bytes=24 * 1024 * 1024),
        name=name,
    )


def shape(*dims, kind=F32):
    return jax.ShapeDtypeStruct(dims, kind)


def local(
    x_prompt,
    z_prompt,
    conv_weight,
    conv_bias,
    xproj_weight,
    dtproj_weight,
    dt_bias,
    decay_rate,
    skip_gain,
    sample_prompt,
    decode_x,
    decode_z,
):
    rows, width = x_prompt.shape
    taps = conv_weight.shape[0]
    places = lax.axis_size("group")
    ring = lax.axis_size("tensor")
    deep = NEAR // 2
    near = [
        [NEAR * a + 2 * ((j + a) % deep) + y for j in range(deep) for y in range(2)]
        for a in range(ring // NEAR)
    ]
    far = [[g[j] for g in near] for j in range(NEAR)]

    tail = x_prompt[rows - (taps - 1) :]
    tails = lax.all_to_all(
        jnp.broadcast_to(tail[None], (places, taps - 1, width)), "group", 0, 0
    )
    columns = xproj_weight.T
    main, cin, nrate, gate, small = call(
        prepare_kernel,
        (
            shape(rows, WIDE),
            shape(rows, width, kind=BF16),
            shape(N, width),
            shape(rows, width),
            shape(24, width),
        ),
        [pltpu.VMEM((rows + 8, width), F32)],
        smem=1,
        inputs=9,
        name="prepare",
    )(
        sample_prompt,
        x_prompt,
        conv_weight,
        conv_bias,
        columns,
        decay_rate.T,
        z_prompt,
        decode_z,
        dt_bias,
        skip_gain,
    )
    part, cin = call(
        project_kernel,
        (shape(NEAR, 16, WIDE, kind=BF16), shape(rows + 16, width, kind=BF16)),
        inputs=7,
        name="project",
    )(tails, main, cin, x_prompt, decode_x, small, columns)

    got = lax.all_to_all(part, "tensor", 0, 0, axis_index_groups=near)
    sums = call(
        near_sum_kernel, shape(ring // NEAR, 16, WIDE, kind=BF16), inputs=1, name="near_sum"
    )(got)
    got = lax.all_to_all(sums, "tensor", 0, 0, axis_index_groups=far)
    sums = call(far_sum_kernel, shape(NEAR, 16, WIDE, kind=BF16), inputs=1, name="far_sum")(got)
    everything = lax.all_to_all(sums, "tensor", 0, 0, axis_index_groups=near)

    send, step, bc, dbc = call(
        step_kernel,
        (
            shape(places, N // 2, 2 * width + 128, kind=BF16),
            shape(rows + 16, width),
            shape(rows, 128),
            shape(8, 128),
        ),
        [
            pltpu.VMEM((rows + 16, R), BF16),
            pltpu.VMEM((rows, width), F32),
            pltpu.VMEM((rows, width), F32),
        ],
        inputs=5,
        name="step",
    )(everything, cin, dtproj_weight, small, nrate)
    states = lax.all_to_all(send, "group", 0, 0)
    y, reach, carry, share, own = call(
        scan_kernel,
        (
            shape(rows, width),
            shape(rows, width),
            shape(KEPT, rows, width, kind=BF16),
            shape(2 * STEPS, N, width, kind=BF16),
            shape(2 * STEPS, width),
        ),
        [pltpu.VMEM((rows, width), F32)],
        inputs=7,
        name="scan",
    )(step, bc, cin, gate, small, nrate, dbc)
    return call(
        finish_kernel,
        (shape(rows, width, kind=BF16), shape(STEPS, 2, width, kind=BF16)),
        [pltpu.VMEM((N, width), F32)],
        inputs=10,
        name="finish",
    )(states, y, reach, carry, bc, gate, nrate, small, share, own)


def solution(mesh):
    placed = (
        P("group", "tensor"),
        P("group", "tensor"),
        P(None, "tensor"),
        P("tensor"),
        P("tensor", None),
        P(None, "tensor"),
        P("tensor"),
        P("tensor", None),
        P("tensor"),
        P("group"),
        P(None, "group", "tensor"),
        P(None, "group", "tensor"),
    )
    return jax.shard_map(
        local,
        mesh=mesh,
        in_specs=placed,
        out_specs=(P("group", "tensor"), P(None, "group", "tensor")),
        check_vma=False,
    )
```

```python
import jax
import jax.numpy as jnp
from jax import lax
from jax.experimental import pallas as pl
from jax.experimental.pallas import tpu as pltpu
from jax.sharding import PartitionSpec as P

N = 16
KEPT = 8
R = 512
STEPS = 4
F32 = jnp.float32
BF16 = jnp.bfloat16
WIDE = 640
BLOCKS = 8
NEAR = 8


def silu(v):
    return v * jax.nn.sigmoid(v)


def softplus(v):
    return jnp.maximum(v, 0.0) + jnp.log1p(jnp.exp(-jnp.abs(v)))


def folded(tile, line):
    lane = lax.broadcasted_iota(jnp.int32, tile.shape, 1)
    four = jnp.concatenate([line[:, 128 * i : 128 * i + 128] for i in range(4)], 0)
    last = pltpu.roll(line[:, R:], 64, 1)
    side = jnp.concatenate([pltpu.roll(four, 64, 1), four, last, jnp.zeros((7, 128), F32)], 0)
    return jnp.where(lane < 64, tile, side)


def unfolded(tile):
    lane = lax.broadcasted_iota(jnp.int32, (4, 128), 1)
    four = jnp.where(lane < 64, pltpu.roll(tile[0:4], 64, 1), tile[4:8])
    return jnp.concatenate([four[i : i + 1] for i in range(4)], 1), pltpu.roll(tile[8:9], 64, 1)


def with_rest(tile):
    lane = lax.broadcasted_iota(jnp.int32, tile.shape, 1)
    row = lax.broadcasted_iota(jnp.int32, tile.shape, 0)
    head = tile.astype(BF16).astype(F32)
    rest = pltpu.roll(tile - head, 2 * N, 1)
    plain = (lax.rem(lane, 64) < 2 * N) | ((lane >= 64) & (row < 8))
    return jnp.where(plain, head, rest)


def joined(block):
    return block + pltpu.roll(block, 128 - 2 * N, 1)


def onto(rows, columns_ref):
    return lax.dot_general(
        rows, columns_ref[...], (((1,), (1,)), ((), ())), preferred_element_type=F32
    )


def prepare_kernel(
    sp_ref, x_ref, w_ref, b_ref, xw_ref, rate_ref, z_ref, dz_ref, db_ref, skip_ref,
    part_ref, cin_ref, nrate_ref, gate_ref, small_ref, ext,
):
    rows, width = x_ref.shape
    ext[0:8, :] = jnp.zeros((8, width), F32)
    ext[8 : 8 + rows, :] = x_ref[...].astype(F32)
    w = w_ref[...].astype(F32)
    taps = w.shape[0]
    bias = b_ref[...].astype(F32).reshape(1, width)
    mixed = bias
    for k in range(taps):
        mixed = mixed + w[k : k + 1] * ext[9 - taps + k : 9 - taps + k + rows, :]
    cin = silu(mixed).astype(BF16)
    cin_ref[...] = cin
    part_ref[:, : R + 2 * N] = onto(cin, xw_ref)
    part_ref[:, R + 2 * N :] = jnp.zeros((rows, WIDE - R - 2 * N), F32)
    nrate_ref[...] = rate_ref[...] * (-1.4426950408889634)
    gate_ref[...] = silu(z_ref[...].astype(F32))
    small_ref[0:8, :] = jnp.concatenate(
        [
            db_ref[...].reshape(1, width),
            skip_ref[...].reshape(1, width),
            bias,
            jnp.zeros((1, width), F32),
            w,
        ],
        0,
    )
    for s in range(2):
        small_ref[16 + s : 17 + s, :] = jnp.full((1, width), sp_ref[s], jnp.int32).astype(F32)
    small_ref[8:16, :] = silu(jnp.concatenate([dz_ref[t].astype(F32) for t in range(STEPS)], 0))


def project_kernel(
    tails_ref, main_ref, cin_ref, x_ref, dx_ref, small_ref, xw_ref, part_ref, all_ref
):
    rows, width = cin_ref.shape
    taps = tails_ref.shape[1] + 1
    place = lax.axis_index("group")
    position = lax.rem(place, BLOCKS)
    bias = small_ref[2:3, :]
    w = small_ref[4 : 4 + taps, :]
    before = tails_ref[jnp.maximum(place - 1, 0)].astype(F32)
    before = jnp.where(position == 0, jnp.zeros_like(before), before)
    near = jnp.concatenate([before, x_ref[0:16, :].astype(F32)[0 : taps - 1]], 0)
    rim = bias
    for k in range(taps):
        rim = rim + w[k : k + 1] * near[k : k + taps - 1]
    first = tails_ref[BLOCKS - 1].astype(F32)
    second = tails_ref[2 * BLOCKS - 1].astype(F32)
    picked = [jnp.where(small_ref[16 + s : 17 + s, :] < 0.5, first, second) for s in range(2)]
    window = [
        jnp.concatenate([picked[0][k : k + 1], picked[1][k : k + 1]], 0) for k in range(taps - 1)
    ] + [dx_ref[t].astype(F32) for t in range(STEPS)]
    lines = []
    for t in range(STEPS):
        mixed = bias
        for k in range(taps):
            mixed = mixed + w[k : k + 1] * window[t + k]
        lines.append(mixed)
    extra = silu(jnp.concatenate([rim, jnp.zeros((8 - (taps - 1), width), F32)] + lines, 0))
    row = lax.broadcasted_iota(jnp.int32, (16, 1), 0)
    start = jnp.where(row < taps - 1, extra, cin_ref[0:16, :].astype(F32))
    all_ref[0:16, :] = start.astype(BF16)
    all_ref[16:rows, :] = cin_ref[16:rows, :]
    all_ref[rows : rows + 16, :] = jnp.concatenate(
        [extra[8:16], jnp.zeros((8, width), F32)], 0
    ).astype(BF16)
    extra = onto(extra.astype(BF16), xw_ref)
    extra = jnp.concatenate([extra, jnp.zeros((16, WIDE - R - 2 * N), F32)], 1)
    for k in range(part_ref.shape[0]):
        mine = main_ref[16 * k : 16 * k + 16, :]
        if k == 0:
            mine = jnp.where(row < taps - 1, extra, mine)
        part_ref[k, :, :R] = mine[:, :R].astype(BF16)
        part_ref[k, :, R:] = folded(mine[:, R:], extra[8 + k : 9 + k]).astype(BF16)


def near_sum_kernel(got_ref, out_ref):
    total = got_ref[0].astype(F32)
    for k in range(1, got_ref.shape[0]):
        total = total + got_ref[k].astype(F32)
    total = total.astype(BF16)
    for k in range(out_ref.shape[0]):
        out_ref[k] = total


def far_sum_kernel(got_ref, out_ref):
    total = (got_ref[0].astype(F32) + got_ref[1].astype(F32)) + (
        got_ref[2].astype(F32) + got_ref[3].astype(F32)
    )
    low = total[:, :R].astype(BF16)
    tile = with_rest(total[:, R:]).astype(BF16)
    for k in range(out_ref.shape[0]):
        out_ref[k, :, :R] = low
        out_ref[k, :, R:] = tile


def parts(value):
    head = value.astype(BF16)
    return head, (value - head.astype(F32)).astype(BF16)


def step_kernel(
    all_ref, cin_ref, dtw_ref, small_ref, nrate_ref,
    msg_ref, step_ref, bc_ref, dbc_ref, low_ref, left_ref, u_ref,
):
    rows, width = u_ref.shape
    lines, tiles = [], []
    for k in range(NEAR):
        at = slice(16 * k, 16 * k + 16)
        tile = all_ref[k, :, R:].astype(F32)
        low_ref[at, :] = all_ref[k, :, :R]
        bc_ref[at, :] = joined(tile)
        line, tile = unfolded(tile)
        lines.append(line)
        tiles.append(tile)
    low_ref[rows : rows + 16, :] = jnp.concatenate(
        lines + [jnp.zeros((8, width), F32)], 0
    ).astype(BF16)
    dbc_ref[...] = joined(jnp.concatenate(tiles, 0))
    step = softplus(
        jnp.dot(low_ref[...], dtw_ref[...], preferred_element_type=F32) + small_ref[0:1, :]
    )
    step_ref[...] = step
    step = step[:rows]
    u_ref[...] = step * cin_ref[0:rows, :].astype(F32)
    down = lax.broadcasted_iota(jnp.int32, (rows, rows), 0)
    over = lax.broadcasted_iota(jnp.int32, (rows, rows), 1)
    after = jnp.where(over > down, 1.0, 0.0).astype(BF16)
    left = sum(jnp.dot(after, part, preferred_element_type=F32) for part in parts(step))
    left_ref[...] = left
    ends = []
    for n in range(N):
        rate = nrate_ref[n : n + 1, :]
        acc = jnp.zeros((16, width), F32)
        for g in range(rows // 16):
            at = slice(16 * g, 16 * g + 16)
            acc = acc + jnp.exp2(rate * left_ref[at, :]) * (bc_ref[at, n : n + 1] * u_ref[at, :])
        ends.append(jnp.sum(acc, axis=0, keepdims=True))
    total = left[0:1] + step[0:1]
    coarse = jnp.concatenate([total[:, 128 * k : 128 * k + 128] for k in range(width // 128)], 0)
    fine = coarse - coarse.astype(BF16).astype(F32)
    ends = jnp.concatenate(ends, 0)
    side = jnp.concatenate([coarse, fine], 0)
    result = jnp.concatenate([ends[:8], ends[8:], side], 1).astype(BF16)
    for k in range(msg_ref.shape[0]):
        msg_ref[k] = result


def scan_kernel(
    step_ref, bc_ref, cin_ref, gate_ref, small_ref, nrate_ref, dbc_ref,
    out_ref, reach_ref, carry_ref, from_ref, dout_ref, u_ref,
):
    rows, width = u_ref.shape
    down = lax.broadcasted_iota(jnp.int32, (rows, rows), 0)
    over = lax.broadcasted_iota(jnp.int32, (rows, rows), 1)
    u_ref[...] = step_ref[0:rows, :] * cin_ref[0:rows, :].astype(F32)
    upto = jnp.where(over <= down, 1.0, 0.0).astype(BF16)
    reach_ref[...] = sum(
        jnp.dot(upto, part, preferred_element_type=F32) for part in parts(step_ref[0:rows, :])
    )

    def carried(g, keep):
        at = pl.ds(pl.multiple_of(16 * g, 16), 16)
        reach = reach_ref[at, :]
        for n in range(KEPT):
            factor = jnp.exp2(nrate_ref[n : n + 1, :] * reach)
            carry_ref[n, at, :] = (bc_ref[at, N + n : N + n + 1] * factor).astype(BF16)
        return keep

    lax.fori_loop(0, rows // 16, carried, 0)
    dbc = jnp.transpose(jnp.concatenate([dbc_ref[...], jnp.zeros((120, 128), F32)], 0))
    nrate = nrate_ref[...]
    skip = small_ref[1:2, :]
    bct = jnp.transpose(bc_ref[...])[0 : 2 * N]

    def group(g, carry):
        h, bc = carry
        at = pl.ds(pl.multiple_of(8 * g, 8), 8)
        d8 = step_ref[at, :]
        u8 = u_ref[at, :]
        values = []
        for j in range(8):
            h = jnp.exp2(nrate * d8[j : j + 1]) * h + bc[0:N, j : j + 1] * u8[j : j + 1]
            values.append(jnp.sum(bc[N : 2 * N, j : j + 1] * h, axis=0, keepdims=True))
        out_ref[at, :] = jnp.concatenate(values, 0)
        return h, pltpu.roll(bc, 120, 1)

    lax.fori_loop(0, rows // 8, group, (jnp.zeros((N, width), F32), bct))
    out_ref[...] = (out_ref[...] + skip * cin_ref[0:rows, :].astype(F32)) * gate_ref[...]
    dec = cin_ref[rows : rows + 16, :].astype(F32)
    own = []
    kept = [jnp.ones((N, width), F32) for _ in range(2)]
    state = [jnp.zeros((N, width), F32) for _ in range(2)]
    for r in range(2 * STEPS):
        s = r % 2
        d = step_ref[rows + r : rows + r + 1, :]
        decay = jnp.exp2(nrate * d)
        kept[s] = decay * kept[s]
        state[s] = decay * state[s] + dbc[0:N, r : r + 1] * (d * dec[r : r + 1])
        c = dbc[N : 2 * N, r : r + 1]
        from_ref[r] = (c * kept[s]).astype(BF16)
        own.append(jnp.sum(c * state[s], axis=0, keepdims=True))
    dout_ref[...] = jnp.concatenate(own, 0) + skip * dec[0 : 2 * STEPS]


def finish_kernel(
    got_ref, y_ref, reach_ref, carry_ref, bc_ref, gate_ref, nrate_ref, small_ref, from_ref, own_ref,
    out_ref, dec_ref, in_ref,
):
    rows, width = y_ref.shape
    place = lax.axis_index("group")
    mine, position = lax.div(place, BLOCKS), lax.rem(place, BLOCKS)
    nrate = nrate_ref[...]
    finals = []
    incoming = jnp.zeros((N, width), F32)
    for p in range(2):
        h = jnp.zeros((N, width), F32)
        for k in range(BLOCKS):
            r = p * BLOCKS + k
            if k > 0:
                incoming = jnp.where((mine == p) & (position == k), h, incoming)
            block = got_ref[r].astype(F32)
            side = block[:, 2 * width :]
            total = side[0:4] + side[4:8]
            total = jnp.concatenate([total[i : i + 1] for i in range(4)], 1)
            end = jnp.concatenate([block[:, :width], block[:, width : 2 * width]], 0)
            h = jnp.exp2(nrate * total) * h + end
        finals.append(h)
    in_ref[...] = incoming

    def group(g, carry):
        at = pl.ds(pl.multiple_of(16 * g, 16), 16)
        s = reach_ref[at, :]
        c = bc_ref[at, :]
        acc = jnp.zeros((16, width), F32)
        for n in range(KEPT):
            acc = acc + in_ref[n : n + 1, :] * carry_ref[n, at, :].astype(F32)
        for n in range(KEPT, N):
            acc = acc + c[:, N + n : N + n + 1] * (
                in_ref[n : n + 1, :] * jnp.exp2(nrate_ref[n : n + 1, :] * s)
            )
        out_ref[at, :] = (y_ref[at, :] + acc * gate_ref[at, :]).astype(BF16)
        return carry

    lax.fori_loop(0, rows // 16, group, 0)
    states = [
        jnp.where(small_ref[16 + s : 17 + s, :] < 0.5, finals[0], finals[1]) for s in range(2)
    ]
    for t in range(STEPS):
        pair = [
            jnp.sum(from_ref[2 * t + s].astype(F32) * states[s], axis=0, keepdims=True) for s in range(2)
        ]
        at = slice(2 * t, 2 * t + 2)
        value = (jnp.concatenate(pair, 0) + own_ref[at, :]) * small_ref[8 + 2 * t : 10 + 2 * t, :]
        dec_ref[t] = value.astype(BF16)


def call(kernel, outs, scratch=(), smem=0, hbm=0, inputs=0, name=None):
    vmem = pl.BlockSpec(memory_space=pltpu.VMEM)
    return pl.pallas_call(
        kernel,
        out_shape=outs,
        in_specs=[pl.BlockSpec(memory_space=pltpu.SMEM)] * smem
        + [pl.BlockSpec(memory_space=pl.ANY)] * hbm
        + [vmem] * inputs,
        out_specs=jax.tree.map(lambda _: vmem, outs),
        scratch_shapes=list(scratch),
        compiler_params=pltpu.CompilerParams(vmem_limit_bytes=24 * 1024 * 1024),
        name=name,
    )


def shape(*dims, kind=F32):
    return jax.ShapeDtypeStruct(dims, kind)


def local(
    x_prompt,
    z_prompt,
    conv_weight,
    conv_bias,
    xproj_weight,
    dtproj_weight,
    dt_bias,
    decay_rate,
    skip_gain,
    sample_prompt,
    decode_x,
    decode_z,
):
    rows, width = x_prompt.shape
    taps = conv_weight.shape[0]
    places = lax.axis_size("group")
    ring = lax.axis_size("tensor")
    deep = NEAR // 2
    near = [
        [NEAR * a + 2 * ((j + a) % deep) + y for j in range(deep) for y in range(2)]
        for a in range(ring // NEAR)
    ]
    far = [[g[j] for g in near] for j in range(NEAR)]

    tail = x_prompt[rows - (taps - 1) :]
    tails = lax.all_to_all(
        jnp.broadcast_to(tail[None], (places, taps - 1, width)), "group", 0, 0
    )
    columns = xproj_weight.T
    main, cin, nrate, gate, small = call(
        prepare_kernel,
        (
            shape(rows, WIDE),
            shape(rows, width, kind=BF16),
            shape(N, width),
            shape(rows, width),
            shape(24, width),
        ),
        [pltpu.VMEM((rows + 8, width), F32)],
        smem=1,
        inputs=9,
        name="prepare",
    )(
        sample_prompt,
        x_prompt,
        conv_weight,
        conv_bias,
        columns,
        decay_rate.T,
        z_prompt,
        decode_z,
        dt_bias,
        skip_gain,
    )
    part, cin = call(
        project_kernel,
        (shape(NEAR, 16, WIDE, kind=BF16), shape(rows + 16, width, kind=BF16)),
        inputs=7,
        name="project",
    )(tails, main, cin, x_prompt, decode_x, small, columns)

    got = lax.all_to_all(part, "tensor", 0, 0, axis_index_groups=near)
    sums = call(
        near_sum_kernel, shape(ring // NEAR, 16, WIDE, kind=BF16), inputs=1, name="near_sum"
    )(got)
    got = lax.all_to_all(sums, "tensor", 0, 0, axis_index_groups=far)
    sums = call(far_sum_kernel, shape(NEAR, 16, WIDE, kind=BF16), inputs=1, name="far_sum")(got)
    everything = lax.all_to_all(sums, "tensor", 0, 0, axis_index_groups=near)

    send, step, bc, dbc = call(
        step_kernel,
        (
            shape(places, N // 2, 2 * width + 128, kind=BF16),
            shape(rows + 16, width),
            shape(rows, 128),
            shape(8, 128),
        ),
        [
            pltpu.VMEM((rows + 16, R), BF16),
            pltpu.VMEM((rows, width), F32),
            pltpu.VMEM((rows, width), F32),
        ],
        inputs=5,
        name="step",
    )(everything, cin, dtproj_weight, small, nrate)
    states = lax.all_to_all(send, "group", 0, 0)
    y, reach, carry, share, own = call(
        scan_kernel,
        (
            shape(rows, width),
            shape(rows, width),
            shape(KEPT, rows, width, kind=BF16),
            shape(2 * STEPS, N, width, kind=BF16),
            shape(2 * STEPS, width),
        ),
        [pltpu.VMEM((rows, width), F32)],
        inputs=7,
        name="scan",
    )(step, bc, cin, gate, small, nrate, dbc)
    return call(
        finish_kernel,
        (shape(rows, width, kind=BF16), shape(STEPS, 2, width, kind=BF16)),
        [pltpu.VMEM((N, width), F32)],
        inputs=10,
        name="finish",
    )(states, y, reach, carry, bc, gate, nrate, small, share, own)


def solution(mesh):
    placed = (
        P("group", "tensor"),
        P("group", "tensor"),
        P(None, "tensor"),
        P("tensor"),
        P("tensor", None),
        P(None, "tensor"),
        P("tensor"),
        P("tensor", None),
        P("tensor"),
        P("group"),
        P(None, "group", "tensor"),
        P(None, "group", "tensor"),
    )
    return jax.shard_map(
        local,
        mesh=mesh,
        in_specs=placed,
        out_specs=(P("group", "tensor"), P(None, "group", "tensor")),
        check_vma=False,
    )
```

```python
import jax
import jax.numpy as jnp
from jax import lax
from jax.experimental import pallas as pl
from jax.experimental.pallas import tpu as pltpu
from jax.sharding import PartitionSpec as P

N = 16
R = 512
STEPS = 4
F32 = jnp.float32
BF16 = jnp.bfloat16
WIDE = 640
BLOCKS = 8
NEAR = 8


def silu(v):
    return v * jax.nn.sigmoid(v)


def softplus(v):
    return jnp.maximum(v, 0.0) + jnp.log1p(jnp.exp(-jnp.abs(v)))


def folded(tile, line):
    lane = lax.broadcasted_iota(jnp.int32, tile.shape, 1)
    four = jnp.concatenate([line[:, 128 * i : 128 * i + 128] for i in range(4)], 0)
    last = pltpu.roll(line[:, R:], 64, 1)
    side = jnp.concatenate([pltpu.roll(four, 64, 1), four, last, jnp.zeros((7, 128), F32)], 0)
    return jnp.where(lane < 64, tile, side)


def unfolded(tile):
    lane = lax.broadcasted_iota(jnp.int32, (4, 128), 1)
    four = jnp.where(lane < 64, pltpu.roll(tile[0:4], 64, 1), tile[4:8])
    return jnp.concatenate([four[i : i + 1] for i in range(4)], 1), pltpu.roll(tile[8:9], 64, 1)


def with_rest(tile):
    lane = lax.broadcasted_iota(jnp.int32, tile.shape, 1)
    row = lax.broadcasted_iota(jnp.int32, tile.shape, 0)
    head = tile.astype(BF16).astype(F32)
    rest = pltpu.roll(tile - head, 2 * N, 1)
    plain = (lax.rem(lane, 64) < 2 * N) | ((lane >= 64) & (row < 8))
    return jnp.where(plain, head, rest)


def joined(block):
    return block + pltpu.roll(block, 128 - 2 * N, 1)


def onto(rows, columns_ref):
    return lax.dot_general(
        rows, columns_ref[...], (((1,), (1,)), ((), ())), preferred_element_type=F32
    )


def prepare_kernel(
    sp_ref, x_ref, w_ref, b_ref, xw_ref, rate_ref, z_ref, dz_ref, db_ref, skip_ref,
    part_ref, cin_ref, nrate_ref, gate_ref, small_ref, ext,
):
    rows, width = x_ref.shape
    ext[0:8, :] = jnp.zeros((8, width), F32)
    ext[8 : 8 + rows, :] = x_ref[...].astype(F32)
    w = w_ref[...].astype(F32)
    taps = w.shape[0]
    bias = b_ref[...].astype(F32).reshape(1, width)
    mixed = bias
    for k in range(taps):
        mixed = mixed + w[k : k + 1] * ext[9 - taps + k : 9 - taps + k + rows, :]
    cin = silu(mixed).astype(BF16)
    cin_ref[...] = cin
    part_ref[:, : R + 2 * N] = onto(cin, xw_ref)
    part_ref[:, R + 2 * N :] = jnp.zeros((rows, WIDE - R - 2 * N), F32)
    nrate_ref[...] = -rate_ref[...]
    gate_ref[...] = silu(z_ref[...].astype(F32))
    small_ref[0:8, :] = jnp.concatenate(
        [
            db_ref[...].reshape(1, width),
            skip_ref[...].reshape(1, width),
            bias,
            jnp.zeros((1, width), F32),
            w,
        ],
        0,
    )
    for s in range(2):
        small_ref[16 + s : 17 + s, :] = jnp.full((1, width), sp_ref[s], jnp.int32).astype(F32)
    small_ref[8:16, :] = silu(jnp.concatenate([dz_ref[t].astype(F32) for t in range(STEPS)], 0))


def project_kernel(
    tails_ref, main_ref, cin_ref, x_ref, dx_ref, small_ref, xw_ref, part_ref, all_ref
):
    rows, width = cin_ref.shape
    taps = tails_ref.shape[1] + 1
    place = lax.axis_index("group")
    position = lax.rem(place, BLOCKS)
    bias = small_ref[2:3, :]
    w = small_ref[4 : 4 + taps, :]
    before = tails_ref[jnp.maximum(place - 1, 0)].astype(F32)
    before = jnp.where(position == 0, jnp.zeros_like(before), before)
    near = jnp.concatenate([before, x_ref[0:16, :].astype(F32)[0 : taps - 1]], 0)
    rim = bias
    for k in range(taps):
        rim = rim + w[k : k + 1] * near[k : k + taps - 1]
    first = tails_ref[BLOCKS - 1].astype(F32)
    second = tails_ref[2 * BLOCKS - 1].astype(F32)
    picked = [jnp.where(small_ref[16 + s : 17 + s, :] < 0.5, first, second) for s in range(2)]
    window = [
        jnp.concatenate([picked[0][k : k + 1], picked[1][k : k + 1]], 0) for k in range(taps - 1)
    ] + [dx_ref[t].astype(F32) for t in range(STEPS)]
    lines = []
    for t in range(STEPS):
        mixed = bias
        for k in range(taps):
            mixed = mixed + w[k : k + 1] * window[t + k]
        lines.append(mixed)
    extra = silu(jnp.concatenate([rim, jnp.zeros((8 - (taps - 1), width), F32)] + lines, 0))
    row = lax.broadcasted_iota(jnp.int32, (16, 1), 0)
    start = jnp.where(row < taps - 1, extra, cin_ref[0:16, :].astype(F32))
    all_ref[0:16, :] = start.astype(BF16)
    all_ref[16:rows, :] = cin_ref[16:rows, :]
    all_ref[rows : rows + 16, :] = jnp.concatenate(
        [extra[8:16], jnp.zeros((8, width), F32)], 0
    ).astype(BF16)
    extra = onto(extra.astype(BF16), xw_ref)
    extra = jnp.concatenate([extra, jnp.zeros((16, WIDE - R - 2 * N), F32)], 1)
    for k in range(part_ref.shape[0]):
        mine = main_ref[16 * k : 16 * k + 16, :]
        if k == 0:
            mine = jnp.where(row < taps - 1, extra, mine)
        part_ref[k, :, :R] = mine[:, :R].astype(BF16)
        part_ref[k, :, R:] = folded(mine[:, R:], extra[8 + k : 9 + k]).astype(BF16)


def near_sum_kernel(got_ref, out_ref):
    total = got_ref[0].astype(F32)
    for k in range(1, got_ref.shape[0]):
        total = total + got_ref[k].astype(F32)
    total = total.astype(BF16)
    for k in range(out_ref.shape[0]):
        out_ref[k] = total


def far_sum_kernel(got_ref, out_ref):
    total = (got_ref[0].astype(F32) + got_ref[1].astype(F32)) + (
        got_ref[2].astype(F32) + got_ref[3].astype(F32)
    )
    low = total[:, :R].astype(BF16)
    tile = with_rest(total[:, R:]).astype(BF16)
    for k in range(out_ref.shape[0]):
        out_ref[k, :, :R] = low
        out_ref[k, :, R:] = tile


def parts(value):
    head = value.astype(BF16)
    return head, (value - head.astype(F32)).astype(BF16)


def step_kernel(
    all_ref, cin_ref, dtw_ref, small_ref, nrate_ref,
    msg_ref, step_ref, bc_ref, u_ref, low_ref, left_ref,
):
    rows, width = u_ref.shape
    for k in range(NEAR):
        at = slice(16 * k, 16 * k + 16)
        low_ref[at, :] = all_ref[k, :, :R]
        bc_ref[at, :] = joined(all_ref[k, :, R:].astype(F32))
    step = softplus(
        jnp.dot(low_ref[...], dtw_ref[...], preferred_element_type=F32) + small_ref[0:1, :]
    )
    step_ref[...] = step
    u_ref[...] = step * cin_ref[0:rows, :].astype(F32)
    down = lax.broadcasted_iota(jnp.int32, (rows, rows), 0)
    over = lax.broadcasted_iota(jnp.int32, (rows, rows), 1)
    after = jnp.where(over > down, 1.0, 0.0).astype(BF16)
    left = sum(jnp.dot(after, part, preferred_element_type=F32) for part in parts(step))
    left_ref[...] = left
    ends = []
    for n in range(N):
        rate = nrate_ref[n : n + 1, :]
        acc = jnp.zeros((16, width), F32)
        for g in range(rows // 16):
            at = slice(16 * g, 16 * g + 16)
            acc = acc + jnp.exp(rate * left_ref[at, :]) * (bc_ref[at, n : n + 1] * u_ref[at, :])
        ends.append(jnp.sum(acc, axis=0, keepdims=True))
    total = left[0:1] + step[0:1]
    coarse = jnp.concatenate([total[:, 128 * k : 128 * k + 128] for k in range(width // 128)], 0)
    fine = coarse - coarse.astype(BF16).astype(F32)
    ends = jnp.concatenate(ends, 0)
    side = jnp.concatenate([coarse, fine], 0)
    result = jnp.concatenate([ends[:8], ends[8:], side], 1).astype(BF16)
    for k in range(msg_ref.shape[0]):
        msg_ref[k] = result


def scan_kernel(
    all_ref, dtw_ref, step_ref, u_ref, bc_ref, cin_ref, gate_ref, small_ref, nrate_ref,
    out_ref, reach_ref, from_ref, dout_ref,
):
    rows, width = u_ref.shape
    down = lax.broadcasted_iota(jnp.int32, (rows, rows), 0)
    over = lax.broadcasted_iota(jnp.int32, (rows, rows), 1)
    upto = jnp.where(over <= down, 1.0, 0.0).astype(BF16)
    reach_ref[...] = sum(
        jnp.dot(upto, part, preferred_element_type=F32) for part in parts(step_ref[0:rows, :])
    )
    pairs = [unfolded(all_ref[k, :, R:].astype(F32)) for k in range(NEAR)]
    low = jnp.concatenate([line for line, _ in pairs] + [jnp.zeros((8, width), F32)], 0)
    dstep = softplus(
        jnp.dot(low.astype(BF16), dtw_ref[...], preferred_element_type=F32) + small_ref[0:1, :]
    )
    dbc = joined(jnp.concatenate([tile for _, tile in pairs], 0))
    dbc = jnp.transpose(jnp.concatenate([dbc, jnp.zeros((120, 128), F32)], 0))
    nrate = nrate_ref[...]
    skip = small_ref[1:2, :]
    bct = jnp.transpose(bc_ref[...])[0 : 2 * N]

    def group(g, carry):
        h, bc = carry
        at = pl.ds(pl.multiple_of(8 * g, 8), 8)
        d8 = step_ref[at, :]
        u8 = u_ref[at, :]
        values = []
        for j in range(8):
            h = jnp.exp(nrate * d8[j : j + 1]) * h + bc[0:N, j : j + 1] * u8[j : j + 1]
            values.append(jnp.sum(bc[N : 2 * N, j : j + 1] * h, axis=0, keepdims=True))
        out_ref[at, :] = jnp.concatenate(values, 0)
        return h, pltpu.roll(bc, 120, 1)

    lax.fori_loop(0, rows // 8, group, (jnp.zeros((N, width), F32), bct))
    out_ref[...] = (out_ref[...] + skip * cin_ref[0:rows, :].astype(F32)) * gate_ref[...]
    dec = cin_ref[rows : rows + 16, :].astype(F32)
    own = []
    kept = [jnp.ones((N, width), F32) for _ in range(2)]
    state = [jnp.zeros((N, width), F32) for _ in range(2)]
    for r in range(2 * STEPS):
        s = r % 2
        d = dstep[r : r + 1]
        decay = jnp.exp(nrate * d)
        kept[s] = decay * kept[s]
        state[s] = decay * state[s] + dbc[0:N, r : r + 1] * (d * dec[r : r + 1])
        c = dbc[N : 2 * N, r : r + 1]
        from_ref[r] = c * kept[s]
        own.append(jnp.sum(c * state[s], axis=0, keepdims=True))
    dout_ref[...] = jnp.concatenate(own, 0) + skip * dec[0 : 2 * STEPS]


def finish_kernel(
    got_ref, y_ref, reach_ref, bc_ref, gate_ref, nrate_ref, small_ref, from_ref, own_ref,
    out_ref, dec_ref, in_ref,
):
    rows, width = y_ref.shape
    place = lax.axis_index("group")
    mine, position = lax.div(place, BLOCKS), lax.rem(place, BLOCKS)
    nrate = nrate_ref[...]
    finals = []
    incoming = jnp.zeros((N, width), F32)
    for p in range(2):
        h = jnp.zeros((N, width), F32)
        for k in range(BLOCKS):
            r = p * BLOCKS + k
            if k > 0:
                incoming = jnp.where((mine == p) & (position == k), h, incoming)
            block = got_ref[r].astype(F32)
            side = block[:, 2 * width :]
            total = side[0:4] + side[4:8]
            total = jnp.concatenate([total[i : i + 1] for i in range(4)], 1)
            end = jnp.concatenate([block[:, :width], block[:, width : 2 * width]], 0)
            h = jnp.exp(nrate * total) * h + end
        finals.append(h)
    in_ref[...] = incoming

    def group(g, carry):
        at = pl.ds(pl.multiple_of(16 * g, 16), 16)
        s = reach_ref[at, :]
        c = bc_ref[at, :]
        acc = jnp.zeros((16, width), F32)
        for n in range(N):
            acc = acc + c[:, N + n : N + n + 1] * (
                in_ref[n : n + 1, :] * jnp.exp(nrate_ref[n : n + 1, :] * s)
            )
        out_ref[at, :] = (y_ref[at, :] + acc * gate_ref[at, :]).astype(BF16)
        return carry

    lax.fori_loop(0, rows // 16, group, 0)
    states = [
        jnp.where(small_ref[16 + s : 17 + s, :] < 0.5, finals[0], finals[1]) for s in range(2)
    ]
    for t in range(STEPS):
        pair = [
            jnp.sum(from_ref[2 * t + s] * states[s], axis=0, keepdims=True) for s in range(2)
        ]
        at = slice(2 * t, 2 * t + 2)
        value = (jnp.concatenate(pair, 0) + own_ref[at, :]) * small_ref[8 + 2 * t : 10 + 2 * t, :]
        dec_ref[t] = value.astype(BF16)


def call(kernel, outs, scratch=(), smem=0, hbm=0, inputs=0, name=None):
    vmem = pl.BlockSpec(memory_space=pltpu.VMEM)
    return pl.pallas_call(
        kernel,
        out_shape=outs,
        in_specs=[pl.BlockSpec(memory_space=pltpu.SMEM)] * smem
        + [pl.BlockSpec(memory_space=pl.ANY)] * hbm
        + [vmem] * inputs,
        out_specs=jax.tree.map(lambda _: vmem, outs),
        scratch_shapes=list(scratch),
        compiler_params=pltpu.CompilerParams(vmem_limit_bytes=24 * 1024 * 1024),
        name=name,
    )


def shape(*dims, kind=F32):
    return jax.ShapeDtypeStruct(dims, kind)


def local(
    x_prompt,
    z_prompt,
    conv_weight,
    conv_bias,
    xproj_weight,
    dtproj_weight,
    dt_bias,
    decay_rate,
    skip_gain,
    sample_prompt,
    decode_x,
    decode_z,
):
    rows, width = x_prompt.shape
    taps = conv_weight.shape[0]
    places = lax.axis_size("group")
    ring = lax.axis_size("tensor")
    deep = NEAR // 2
    near = [
        [NEAR * a + 2 * ((j + a) % deep) + y for j in range(deep) for y in range(2)]
        for a in range(ring // NEAR)
    ]
    far = [[g[j] for g in near] for j in range(NEAR)]

    tail = x_prompt[rows - (taps - 1) :]
    tails = lax.all_to_all(
        jnp.broadcast_to(tail[None], (places, taps - 1, width)), "group", 0, 0
    )
    columns = xproj_weight.T
    main, cin, nrate, gate, small = call(
        prepare_kernel,
        (
            shape(rows, WIDE),
            shape(rows, width, kind=BF16),
            shape(N, width),
            shape(rows, width),
            shape(24, width),
        ),
        [pltpu.VMEM((rows + 8, width), F32)],
        smem=1,
        inputs=9,
        name="prepare",
    )(
        sample_prompt,
        x_prompt,
        conv_weight,
        conv_bias,
        columns,
        decay_rate.T,
        z_prompt,
        decode_z,
        dt_bias,
        skip_gain,
    )
    part, cin = call(
        project_kernel,
        (shape(NEAR, 16, WIDE, kind=BF16), shape(rows + 16, width, kind=BF16)),
        inputs=7,
        name="project",
    )(tails, main, cin, x_prompt, decode_x, small, columns)

    got = lax.all_to_all(part, "tensor", 0, 0, axis_index_groups=near)
    sums = call(
        near_sum_kernel, shape(ring // NEAR, 16, WIDE, kind=BF16), inputs=1, name="near_sum"
    )(got)
    got = lax.all_to_all(sums, "tensor", 0, 0, axis_index_groups=far)
    sums = call(far_sum_kernel, shape(NEAR, 16, WIDE, kind=BF16), inputs=1, name="far_sum")(got)
    everything = lax.all_to_all(sums, "tensor", 0, 0, axis_index_groups=near)

    send, step, bc, u = call(
        step_kernel,
        (
            shape(places, N // 2, 2 * width + 128, kind=BF16),
            shape(rows, width),
            shape(rows, 128),
            shape(rows, width),
        ),
        [pltpu.VMEM((rows, R), BF16), pltpu.VMEM((rows, width), F32)],
        inputs=5,
        name="step",
    )(everything, cin, dtproj_weight, small, nrate)
    states = lax.all_to_all(send, "group", 0, 0)
    y, reach, share, own = call(
        scan_kernel,
        (
            shape(rows, width),
            shape(rows, width),
            shape(2 * STEPS, N, width),
            shape(2 * STEPS, width),
        ),
        inputs=9,
        name="scan",
    )(everything, dtproj_weight, step, u, bc, cin, gate, small, nrate)
    return call(
        finish_kernel,
        (shape(rows, width, kind=BF16), shape(STEPS, 2, width, kind=BF16)),
        [pltpu.VMEM((N, width), F32)],
        inputs=9,
        name="finish",
    )(states, y, reach, bc, gate, nrate, small, share, own)


def solution(mesh):
    placed = (
        P("group", "tensor"),
        P("group", "tensor"),
        P(None, "tensor"),
        P("tensor"),
        P("tensor", None),
        P(None, "tensor"),
        P("tensor"),
        P("tensor", None),
        P("tensor"),
        P("group"),
        P(None, "group", "tensor"),
        P(None, "group", "tensor"),
    )
    return jax.shard_map(
        local,
        mesh=mesh,
        in_specs=placed,
        out_specs=(P("group", "tensor"), P(None, "group", "tensor")),
        check_vma=False,
    )
```
